256 devices in a mesh: row: 32 (over y_hi, z, core), col: 8 (over x, y_lo).
Axes of the slice: x: 4, y: 4 (y_hi: 2, y_lo: 2; y = y_hi * 2 + y_lo), z: 8, core: 2. Of those that a mesh axis runs over, the one named last changes fastest.
Arguments:
- tokens: bfloat16 [256, 128, 384], P('row', 'col'), may hold values from -6 to 6
- timestep: int32 [1], replicated, may hold values from 0 to 999
- time_weight: float32 [256, 384], replicated, may hold values from -0.375 to 0.375
- query0: bfloat16 [384, 384], replicated, may hold values from -0.3125 to 0.3125
- key0: bfloat16 [384, 384], replicated, may hold values from -0.3125 to 0.3125
- value0: bfloat16 [384, 384], replicated, may hold values from -0.3125 to 0.3125
- out0: bfloat16 [384, 384], replicated, may hold values from -0.3125 to 0.3125
- merge_one: bfloat16 [1536, 768], replicated, may hold values from -0.15625 to 0.15625
- merge_two: bfloat16 [3072, 1536], P('row', 'col'), may hold values from -0.109375 to 0.109375
- gain_two: float32 [1536], replicated, may hold values from 0.25 to 1.75
- query2: bfloat16 [1536, 1536], P(None, 'col'), may hold values from -0.3125 to 0.3125
- key2: bfloat16 [1536, 1536], P(None, 'col'), may hold values from -0.3125 to 0.3125
- value2: bfloat16 [1536, 1536], P(None, 'col'), may hold values from -0.15625 to 0.15625
- out2: bfloat16 [1536, 1536], P('col'), may hold values from -0.15625 to 0.15625
- split_two: bfloat16 [1536, 3072], P('row', 'col'), may hold values from -0.15625 to 0.15625
- split_one: bfloat16 [768, 1536], replicated, may hold values from -0.21875 to 0.21875
Outputs:
- out_tokens: bfloat16 [256, 128, 384], P('row', 'col')
The draws below stay inside these ranges and needn't reach their ends.
All inputs are finite; a program needn't handle non-finite values.
Results may differ from the reference program's by a relative error of at most 0.035.
Values may be sent and summed in bfloat16 or wider, within the bound.
No kernel may reach another device: no remote copies, remote signals or barrier semaphores. Data moves between devices by JAX's collectives and lax.ppermute only.
A program may use at most 64 MiB of HBM per device.

```python
import math
import jax
import jax.numpy as jnp
from jax import lax

D0 = 384
D1 = 768
D2 = 1536
HEAD = 64
RADIUS = 3
FREQ = 256
IMG_R = 256
IMG_C = 128


def steps_of(own_key, dims, split, least, high):
    loudness, own = 1.0, jax.random.fold_in(own_key, 6)
    for dim, shards_of in split:
        steps = jnp.exp(jax.random.uniform(jax.random.fold_in(own, dim), (shards_of,), jnp.float32, least / len(split), high / len(split)))
        loudness = loudness * jnp.repeat(steps, dims[dim] // shards_of).reshape([-1 if axis == dim else 1 for axis in range(len(dims))])
    return loudness


def gaussian(own_key, shape, scale, limit, shards=(), kind=jnp.bfloat16):
    factor_of = steps_of(own_key, shape, shards, -0.22, 0.18) if shards else 1.0
    array = jax.random.normal(own_key, shape, jnp.float32) * scale * factor_of
    return jnp.minimum(jnp.maximum(array, -limit), limit).astype(kind)


def setup_inputs(seed: int = 0) -> dict:
    streams_of = jax.random.split(jax.random.key(seed), 17)
    return {
        "tokens": gaussian(streams_of[0], (IMG_R, IMG_C, D0), 1.0, 6.0, ((0, 32), (1, 8))),
        "timestep": jax.random.randint(streams_of[1], (1,), 0, 1000).astype(jnp.int32),
        "time_weight": gaussian(streams_of[2], (FREQ, D0), FREQ ** -0.5, 0.375, (), jnp.float32),
        "query0": gaussian(streams_of[3], (D0, D0), D0 ** -0.5, 0.3125),
        "key0": gaussian(streams_of[4], (D0, D0), D0 ** -0.5, 0.3125),
        "value0": gaussian(streams_of[5], (D0, D0), D0 ** -0.5, 0.3125),
        "out0": gaussian(streams_of[6], (D0, D0), D0 ** -0.5, 0.3125),
        "merge_one": gaussian(streams_of[7], (4 * D0, D1), (4 * D0) ** -0.5, 0.15625),
        "merge_two": gaussian(streams_of[8], (4 * D1, D2), (4 * D1) ** -0.5, 0.109375, ((0, 32), (1, 8))),
        "gain_two": jnp.clip(1.0 + 0.15 * jax.random.normal(streams_of[9], (D2,), jnp.float32), 0.25, 1.75),
        "query2": gaussian(streams_of[10], (D2, D2), (D2 // 4) ** -0.5, 0.3125, ((1, 8),)),
        "key2": gaussian(streams_of[11], (D2, D2), (D2 // 4) ** -0.5, 0.3125, ((1, 8),)),
        "value2": gaussian(streams_of[12], (D2, D2), D2 ** -0.5, 0.15625, ((1, 8),)),
        "out2": gaussian(streams_of[13], (D2, D2), D2 ** -0.5, 0.15625, ((0, 8),)),
        "split_two": gaussian(streams_of[14], (D2, 4 * D1), D2 ** -0.5, 0.15625, ((0, 32), (1, 8))),
        "split_one": gaussian(streams_of[15], (D1, 4 * D0), D1 ** -0.5, 0.21875),
    }


epsilon = 1e-06

def time_features(timestep, count):
    half_count = count // 2
    ladder = jnp.arange(half_count, dtype=jnp.float32)
    freqs = jnp.exp(-math.log(10000.0) * ladder / half_count)
    angles = timestep.astype(jnp.float32)[0] * freqs
    return jnp.concatenate([jnp.cos(angles), jnp.sin(angles)])

def rms_norm(values):
    floats = values.astype(jnp.float32)
    return floats * lax.rsqrt(lax.optimization_barrier(jnp.mean(floats * floats, axis=-1, keepdims=True)) + epsilon)

def group_quads(values):
    height, breadth, feature = values.shape
    return values.reshape(height // 2, 2, breadth // 2, 2, feature).transpose(0, 2, 1, 3, 4).reshape(height // 2, breadth // 2, 4 * feature)

def ungroup(values):
    height, breadth, feature = values.shape
    inner = feature // 4
    return values.reshape(height, breadth, 2, 2, inner).transpose(0, 2, 1, 3, 4).reshape(2 * height, 2 * breadth, inner)

def project(values, weight):
    return jnp.dot(values, weight, preferred_element_type=jnp.float32)

def neighbour_attention(queries, keys_ext, values_ext, valid_rows, valid_cols):
    height, breadth, feature = queries.shape
    head_count = feature // HEAD
    factor = 1.0 / math.sqrt(HEAD)
    window = 2 * RADIUS + 1
    query_heads = queries.reshape(height, breadth, head_count, HEAD).astype(jnp.float32)
    score_list = []
    for offset_row in range(window):
        for offset_col in range(window):
            key_block = keys_ext[offset_row:offset_row + height, offset_col:offset_col + breadth]
            key_block = key_block.reshape(height, breadth, head_count, HEAD).astype(jnp.float32)
            scores = jnp.einsum('rchd,rchd->rch', query_heads, key_block) * factor
            inside = valid_rows[offset_row:offset_row + height][:, None] & valid_cols[offset_col:offset_col + breadth][None, :]
            score_list.append(jnp.where(inside[:, :, None], scores, -1e+30))
    weights = jax.nn.softmax(jnp.stack(score_list), axis=0).astype(jnp.bfloat16)
    summed = jnp.zeros((height, breadth, head_count, HEAD), jnp.float32)
    position = 0
    for offset_row in range(window):
        for offset_col in range(window):
            value_block = values_ext[offset_row:offset_row + height, offset_col:offset_col + breadth]
            value_block = value_block.reshape(height, breadth, head_count, HEAD).astype(jnp.float32)
            summed = summed + weights[position][..., None].astype(jnp.float32) * value_block
            position += 1
    return summed.astype(jnp.bfloat16).reshape(height, breadth, feature)

def reference(tokens, timestep, time_weight, query0, key0, value0, out0, merge_one, merge_two, gain_two, query2, key2, value2, out2, split_two, split_one):
    height, breadth, feature = tokens.shape
    condition = jnp.dot(time_features(timestep, FREQ)[None, :], time_weight, precision=lax.Precision.HIGHEST)[0]
    normed = (rms_norm(tokens) * (1.0 + condition)).astype(jnp.bfloat16)
    flat_in = normed.reshape(-1, feature)
    queries = project(flat_in, query0).astype(jnp.bfloat16).reshape(height, breadth, feature)
    keys = project(flat_in, key0).astype(jnp.bfloat16).reshape(height, breadth, feature)
    values = project(flat_in, value0).astype(jnp.bfloat16).reshape(height, breadth, feature)
    pad_spec = ((RADIUS, RADIUS), (RADIUS, RADIUS), (0, 0))
    keys_ext = jnp.pad(keys, pad_spec)
    values_ext = jnp.pad(values, pad_spec)
    row_ladder = jnp.arange(height + 2 * RADIUS)
    col_ladder = jnp.arange(breadth + 2 * RADIUS)
    valid_rows = (row_ladder >= RADIUS) & (row_ladder < height + RADIUS)
    valid_cols = (col_ladder >= RADIUS) & (col_ladder < breadth + RADIUS)
    attended = neighbour_attention(queries, keys_ext, values_ext, valid_rows, valid_cols)
    resid0 = (tokens.astype(jnp.float32) + project(attended.reshape(-1, feature), out0).reshape(height, breadth, feature)).astype(jnp.bfloat16)
    level1 = project(group_quads(resid0).reshape(-1, 4 * feature), merge_one).astype(jnp.bfloat16)
    level1 = level1.reshape(height // 2, breadth // 2, -1)
    grouped = group_quads(level1)
    middle = project(grouped.reshape(-1, grouped.shape[-1]), merge_two).astype(jnp.bfloat16)
    normed2 = (rms_norm(middle) * gain_two).astype(jnp.bfloat16)
    heads2 = middle.shape[1] // HEAD

    def split_heads(weight):
        return project(normed2, weight).astype(jnp.bfloat16).reshape(-1, heads2, HEAD).transpose(1, 0, 2)

    def head_attention(triple):
        query_head, key_head, value_head = triple
        scores = project(query_head, key_head.T) / math.sqrt(HEAD)
        weights = jax.nn.softmax(scores, axis=-1).astype(jnp.bfloat16)
        return project(weights, value_head).astype(jnp.bfloat16)
    attended2 = lax.map(head_attention, (split_heads(query2), split_heads(key2), split_heads(value2)))
    attended2 = attended2.transpose(1, 0, 2).reshape(-1, heads2 * HEAD)
    lifted_mid = (middle.astype(jnp.float32) + project(attended2, out2)).astype(jnp.bfloat16)
    up_one = project(lifted_mid, split_two).reshape(height // 4, breadth // 4, -1)
    lifted1 = (level1.astype(jnp.float32) + ungroup(up_one)).astype(jnp.bfloat16)
    up_zero = project(lifted1.reshape(-1, lifted1.shape[-1]), split_one).reshape(height // 2, breadth // 2, -1)
    return (resid0.astype(jnp.float32) + ungroup(up_zero)).astype(jnp.bfloat16)
```

```python
import functools
import math

import jax
import jax.numpy as jnp
from jax import lax
from jax.experimental import pallas as pl
from jax.experimental.pallas import tpu as pltpu
from jax.sharding import Mesh, PartitionSpec as P

HEAD = 64
RADIUS = 3
FREQ = 256
EPSILON = 1e-06
LOWEST = -1e30

ROW = ("yh", "z", "k")
COL = ("x", "yl")
BF = jnp.bfloat16
F32 = jnp.float32
MIB = 1 << 20


def shift(axis, step):
    count = lax.axis_size(axis)
    pairs = [(i, i + 1) for i in range(count - 1)]
    return pairs if step > 0 else [(b, a) for a, b in pairs]


def swap(axis):
    return [(0, 1), (1, 0)]


def exchange(block, axis):
    return lax.all_to_all(block, axis, split_axis=0, concat_axis=0, tiled=True)


def in_order(block, axis):
    other = lax.ppermute(block, axis, swap(axis))
    first = lax.axis_index(axis) == 0
    low = jnp.where(first, block, other)
    high = jnp.where(first, other, block)
    return jnp.concatenate([low, high], axis=0)


def copies(block, count):
    return jnp.broadcast_to(block[None], (count,) + block.shape).reshape(
        (count * block.shape[0],) + block.shape[1:]
    )


def dot(a, b):
    return jnp.dot(a, b, preferred_element_type=F32)


def dot_nt(a, b):
    return lax.dot_general(a, b, (((1,), (1,)), ((), ())), preferred_element_type=F32)


def call(body, out_shape, args, us, smem=(), name=None):
    specs = [
        pl.BlockSpec(memory_space=pltpu.SMEM if i in smem else pltpu.VMEM)
        for i in range(len(args))
    ]
    many = isinstance(out_shape, (tuple, list))
    out_specs = (
        tuple(pl.BlockSpec(memory_space=pltpu.VMEM) for _ in out_shape)
        if many
        else pl.BlockSpec(memory_space=pltpu.VMEM)
    )
    return pl.pallas_call(
        body,
        out_shape=out_shape,
        in_specs=specs,
        out_specs=out_specs,
        compiler_params=pltpu.CompilerParams(vmem_limit_bytes=24 * MIB),
        cost_estimate=pl.CostEstimate(
            flops=int(us * 1e9), bytes_accessed=int(us * 3e6), transcendentals=0
        ),
        name=name,
    )(*args)


def place_of(order):
    pos1, pos2, mid = order // 32, (order // 8) % 4, order % 8
    row = (mid // 4) * 4 + (pos2 // 2) * 2 + pos1 // 2
    col = (mid % 4) * 4 + (pos2 % 2) * 2 + pos1 % 2
    return row, col


def finest_kernel(
    where, ext, top, bottom, scale, wq, wk, wv, wo, merge, resid_out, level1_out, band_out
):
    tokens = jnp.concatenate([top[...], ext[...], bottom[...]], axis=0)
    floats = tokens.astype(F32).reshape(448, 384)
    mean = jnp.mean(floats * floats, axis=1, keepdims=True)
    normed = (floats * lax.rsqrt(mean + EPSILON) * scale[...]).astype(BF)
    keys = dot(normed, wk[...]).astype(BF)
    values = dot(normed, wv[...]).astype(BF)

    row, col = place_of(lax.broadcasted_iota(jnp.int32, (128, 448), 0))
    place = lax.broadcasted_iota(jnp.int32, (128, 448), 1)
    key_row, slot = place // 32 - RADIUS, place % 32
    key_col = jnp.where(slot < 16, slot, jnp.where(slot < 24, slot - 24, slot - 8))
    pick = ((key_row == row) & (slot == col)).astype(F32).astype(BF)
    mine = dot(pick, floats.astype(BF))
    queries = dot(dot(pick, normed).astype(BF), wq[...]).astype(BF)

    global_row, global_col = key_row + where[0], key_col + where[1]
    inside = (jnp.abs(key_row - row) <= RADIUS) & (jnp.abs(key_col - col) <= RADIUS)
    inside &= (global_row >= 0) & (global_row < where[2])
    inside &= (global_col >= 0) & (global_col < where[3])
    bias = jnp.where(inside, 0.0, LOWEST)

    lane = lax.broadcasted_iota(jnp.int32, (1, 128), 1)
    low = (lane < HEAD).astype(F32).astype(BF)
    high = (lane >= HEAD).astype(F32).astype(BF)
    blocks = []
    for pair in range(3):
        cut = slice(128 * pair, 128 * pair + 128)
        outs = []
        for half in (low, high):
            scores = dot_nt(queries[:, cut] * half, keys[:, cut]) * (1.0 / math.sqrt(HEAD)) + bias
            exps = jnp.exp(scores - jnp.max(scores, axis=1, keepdims=True))
            weights = (exps / jnp.sum(exps, axis=1, keepdims=True)).astype(BF)
            outs.append(dot(weights, values[:, cut]))
        blocks.append(jnp.where(lane < HEAD, outs[0], outs[1]))
    attended = jnp.concatenate(blocks, axis=1).astype(BF)
    resid = (mine + dot(attended, wo[...])).astype(BF)
    resid_out[...] = resid
    level1 = jnp.zeros((32, 768), F32)
    for pos in range(4):
        level1 += dot(resid[32 * pos : 32 * pos + 32], merge[384 * pos : 384 * pos + 384, :])
    level1_out[...] = level1.astype(BF)
    grouped = jnp.concatenate([level1[8 * pos : 8 * pos + 8] for pos in range(4)], axis=1)
    band_out[...] = jnp.concatenate([grouped] * 8, axis=0).astype(BF)


def middle_kernel(band, weight, mid_out, copies_out):
    blocks = [
        weight[((k * 8 + z) * 2 + yh) * 96 : ((k * 8 + z) * 2 + yh) * 96 + 96, :]
        for yh in range(2)
        for z in range(8)
        for k in range(2)
    ]
    mid = dot(band[...], jnp.concatenate(blocks, axis=0)).astype(BF)
    mid_out[...] = mid
    copies_out[...] = jnp.concatenate([mid] * 8, axis=0)


def project_kernel(mids, gain, wq, wk, wv, q_out, kv_out):
    parts = [mids[64 * i : 64 * i + 64, :].astype(F32) for i in range(8)]
    total = jnp.zeros((64, 1), F32)
    for part in parts:
        total += jnp.sum(part * part, axis=1, keepdims=True)
    inverse = lax.rsqrt(total * (1.0 / 1536.0) + EPSILON)
    sums = [jnp.zeros((64, 192), F32) for _ in range(3)]
    for i, part in enumerate(parts):
        normed = (part * inverse * gain[i : i + 1, :]).astype(BF)
        for j, weight in enumerate((wq, wk, wv)):
            sums[j] += dot(normed, weight[192 * i : 192 * i + 192, :])
    queries, keys, values = sums
    q_out[...] = queries.astype(BF)
    both = jnp.concatenate([keys, values[:, 128:192], values[:, 0:128]], axis=1).astype(BF)
    kv_out[...] = jnp.concatenate([both] * 8, axis=0)


def attend_kernel(q_own, q_other, kv, own_out, other_out):
    queries = jnp.concatenate([q_own[...], q_other[...]], axis=0)
    lane = lax.broadcasted_iota(jnp.int32, (1, 128), 1)
    low = (lane < HEAD).astype(F32).astype(BF)
    high = (lane >= HEAD).astype(F32).astype(BF)
    first = queries[:, 0:128]
    third = jnp.concatenate([queries[:, 128:192], jnp.zeros((128, HEAD), BF)], axis=1)
    stats = jnp.zeros((128, 128), F32)
    nums = []
    for head in range(3):
        query = (first * low, first * high, third)[head]
        keys = kv[:, 128:256] if head == 2 else kv[:, 0:128]
        values = kv[:, 128:256] if head == 2 else kv[:, 256:384]
        scores = dot_nt(query, keys) * (1.0 / math.sqrt(HEAD))
        top = jnp.max(scores, axis=1, keepdims=True)
        exps = jnp.exp(scores - top)
        total = jnp.sum(exps, axis=1, keepdims=True)
        nums.append(dot(exps.astype(BF), values))
        stats = jnp.where(lane == head, top, stats)
        stats = jnp.where(lane == 8 + head, total, stats)
    result = jnp.concatenate(
        [jnp.where(lane < HEAD, nums[0], nums[1]), jnp.where(lane < HEAD, stats, nums[2])], axis=1
    )
    own_out[...] = result[0:64]
    other_out[...] = result[64:128]


def combine_kernel(mine, theirs, out2, parts_out):
    a, b = mine[...], theirs[...]
    factors = []
    for head in range(3):
        top_a, top_b = a[:, 128 + head : 129 + head], b[:, 128 + head : 129 + head]
        sum_a, sum_b = a[:, 136 + head : 137 + head], b[:, 136 + head : 137 + head]
        top = jnp.maximum(top_a, top_b)
        fade_a, fade_b = jnp.exp(top_a - top), jnp.exp(top_b - top)
        whole = 1.0 / (sum_a * fade_a + sum_b * fade_b)
        factors.append((fade_a * whole, fade_b * whole))
    lane = lax.broadcasted_iota(jnp.int32, (1, 128), 1)
    first_a = jnp.where(lane < HEAD, factors[0][0], factors[1][0])
    first_b = jnp.where(lane < HEAD, factors[0][1], factors[1][1])
    pair = (a[:, 0:128] * first_a + b[:, 0:128] * first_b).astype(BF)
    last = (a[:, 192:256] * factors[2][0] + b[:, 192:256] * factors[2][1]).astype(BF)
    result = dot(pair, out2[0:128, :]) + dot(last, out2[128:192, :])
    parts_out[...] = jnp.concatenate(
        [result[:, 192 * i : 192 * i + 192] for i in range(8)], axis=0
    ).astype(BF)


def lift_kernel(parts, mid, weight, up_out):
    total = mid[...].astype(F32)
    sums = jnp.zeros((64, 192), F32)
    for i in range(8):
        sums += parts[64 * i : 64 * i + 64, :].astype(F32)
    lifted = (total + sums).astype(BF)
    for i in range(8):
        up_out[:, 384 * i : 384 * i + 384] = dot(
            lifted, weight[192 * i : 192 * i + 192, :]
        ).astype(BF)


def last_kernel(parts, level1, resid, split, out):
    up = jnp.sum(parts[...].astype(F32).reshape(8, 8, 3072), axis=0)
    spread = jnp.concatenate([up[:, 768 * pos : 768 * pos + 768] for pos in range(4)], axis=0)
    lifted = (level1[...].astype(F32) + spread).astype(BF)
    zero = dot(lifted, split[...])
    rise = jnp.concatenate([zero[:, 384 * pos : 384 * pos + 384] for pos in range(4)], axis=0)
    result = (resid[...].astype(F32) + rise).astype(BF)
    place = lax.broadcasted_iota(jnp.int32, (128, 128), 0)
    row, col = place_of(lax.broadcasted_iota(jnp.int32, (128, 128), 1))
    back = ((place // 16 == row) & (place % 16 == col)).astype(F32).astype(BF)
    out[...] = dot(back, result).reshape(8, 16, 384).astype(BF)


def time_features(timestep, count):
    half_count = count // 2
    ladder = jnp.arange(half_count, dtype=F32)
    freqs = jnp.exp(-math.log(10000.0) * ladder / half_count)
    angles = timestep.astype(F32)[0] * freqs
    return jnp.concatenate([jnp.cos(angles), jnp.sin(angles)])


def on_device(
    tokens,
    timestep,
    time_weight,
    query0,
    key0,
    value0,
    out0,
    merge_one,
    merge_two,
    gain_two,
    query2,
    key2,
    value2,
    out2,
    split_two,
    split_one,
):
    shaped = jax.ShapeDtypeStruct
    left = lax.ppermute(tokens[:, 8:16], COL, shift(COL, 1))
    right = lax.ppermute(tokens[:, 0:8], COL, shift(COL, -1))
    ext = jnp.concatenate([tokens, left, right], axis=1)
    top = lax.ppermute(ext[8 - RADIUS : 8], ROW, shift(ROW, 1))
    bottom = lax.ppermute(ext[0:RADIUS], ROW, shift(ROW, -1))

    merge_block = exchange(copies(in_order(merge_two, "yh"), 8), "z")
    merge_block = lax.all_gather(merge_block, "k", axis=0, tiled=True)

    perm = []
    for row in range(32):
        for col in range(8):
            yh, k = (row % 4) // 2, row % 2
            perm.append((row * 8 + col, ((yh * 8 + col) * 2 + k) * 8 + row // 4))
    split_block = lax.ppermute(split_two, ROW + COL, perm)
    split_block = lax.all_gather(split_block, "k", axis=0, tiled=True)
    split_block = in_order(split_block, "yh")
    split_block = lax.all_gather(split_block, "z", axis=0, tiled=True)

    condition = jnp.dot(
        time_features(timestep, FREQ)[None, :], time_weight, precision=lax.Precision.HIGHEST
    )
    where = jnp.stack(
        [
            lax.axis_index(ROW) * 8,
            lax.axis_index(COL) * 16,
            jnp.int32(8 * lax.axis_size(ROW)),
            jnp.int32(16 * lax.axis_size(COL)),
        ]
    ).astype(jnp.int32)
    resid, level1, band = call(
        finest_kernel,
        (shaped((128, 384), BF), shaped((32, 768), BF), shaped((64, 3072), BF)),
        (where, ext, top, bottom, 1.0 + condition, query0, key0, value0, out0, merge_one),
        6,
        smem=(0,),
        name="finest",
    )
    band = exchange(band, COL)
    mid, mids = call(
        middle_kernel,
        (shaped((64, 192), BF), shaped((512, 192), BF)),
        (band, merge_block),
        2,
        name="middle",
    )
    mids = exchange(mids, COL)
    q, kv = call(
        project_kernel,
        (shaped((64, 192), BF), shaped((512, 384), BF)),
        (mids, gain_two.reshape(8, 192), query2, key2, value2),
        2,
        name="project",
    )
    q_other = lax.ppermute(q, "yh", swap("yh"))
    kv = exchange(kv, "z")
    kv = lax.all_gather(kv, "k", axis=0, tiled=True)
    own, other = call(
        attend_kernel,
        (shaped((64, 256), F32), shaped((64, 256), F32)),
        (q, q_other, kv),
        3,
        name="attend",
    )
    theirs = lax.ppermute(other, "yh", swap("yh"))
    parts = call(combine_kernel, shaped((512, 192), BF), (own, theirs, out2), 1, name="combine")
    parts = exchange(parts, COL)
    up = call(lift_kernel, shaped((64, 3072), BF), (parts, mid, split_block), 1, name="lift")
    up = exchange(up, COL)
    return call(
        last_kernel, shaped((8, 16, 384), BF), (up, level1, resid, split_one), 2, name="last"
    )


def solution(mesh):
    fine = Mesh(mesh.devices.reshape(2, 8, 2, 4, 2), ROW + COL)
    in_specs = (
        P(ROW, COL, None),
        P(),
        P(),
        P(),
        P(),
        P(),
        P(),
        P(),
        P(ROW, COL),
        P(),
        P(None, COL),
        P(None, COL),
        P(None, COL),
        P(COL, None),
        P(ROW, COL),
        P(),
    )
    return jax.shard_map(
        on_device, mesh=fine, in_specs=in_specs, out_specs=P(ROW, COL, None), check_vma=False
    )
```

```python
import functools
import math

import jax
import jax.numpy as jnp
from jax import lax
from jax.experimental import pallas as pl
from jax.experimental.pallas import tpu as pltpu
from jax.sharding import Mesh, PartitionSpec as P

HEAD = 64
RADIUS = 3
FREQ = 256
EPSILON = 1e-06
LOWEST = -1e30

ROW = ("yh", "z", "k")
COL = ("x", "yl")
BF = jnp.bfloat16
F32 = jnp.float32
MIB = 1 << 20


def shift(axis, step):
    count = lax.axis_size(axis)
    pairs = [(i, i + 1) for i in range(count - 1)]
    return pairs if step > 0 else [(b, a) for a, b in pairs]


def swap(axis):
    return [(0, 1), (1, 0)]


def exchange(block, axis):
    return lax.all_to_all(block, axis, split_axis=0, concat_axis=0, tiled=True)


def in_order(block, axis):
    other = lax.ppermute(block, axis, swap(axis))
    first = lax.axis_index(axis) == 0
    low = jnp.where(first, block, other)
    high = jnp.where(first, other, block)
    return jnp.concatenate([low, high], axis=0)


def copies(block, count):
    return jnp.broadcast_to(block[None], (count,) + block.shape).reshape(
        (count * block.shape[0],) + block.shape[1:]
    )


def dot(a, b):
    return jnp.dot(a, b, preferred_element_type=F32)


def dot_nt(a, b):
    return lax.dot_general(a, b, (((1,), (1,)), ((), ())), preferred_element_type=F32)


def call(body, out_shape, args, us, smem=(), far=(), through=(), scratch=(), name=None, vmem=16, out_far=()):
    ins, outs = len(args), len(out_shape)
    specs = [
        pl.BlockSpec(
            memory_space=pltpu.SMEM if i in smem else pltpu.HBM if i in far else pltpu.VMEM
        )
        for i in range(ins)
    ] + [pl.BlockSpec(memory_space=pl.ANY) for _ in through]
    out_specs = tuple(
        pl.BlockSpec(memory_space=pltpu.HBM if i in out_far else pltpu.VMEM) for i in range(outs)
    ) + tuple(
        pl.BlockSpec(memory_space=pl.ANY) for _ in through
    )
    out_shape = tuple(
        pltpu.HBM(a.shape, a.dtype) if i in out_far else a for i, a in enumerate(out_shape)
    ) + tuple(
        jax.ShapeDtypeStruct(a.shape, a.dtype) for a in through
    )
    args = tuple(args) + tuple(through)
    count = len(through)

    def kernel(*refs):
        body(*refs[:ins], *refs[ins + count : ins + count + outs], *refs[ins + 2 * count + outs :])

    result = pl.pallas_call(
        kernel,
        out_shape=out_shape,
        in_specs=specs,
        out_specs=out_specs,
        scratch_shapes=tuple(scratch),
        input_output_aliases={ins + i: outs + i for i in range(count)},
        compiler_params=pltpu.CompilerParams(vmem_limit_bytes=vmem * MIB),
        cost_estimate=pl.CostEstimate(
            flops=int(us * 1e9), bytes_accessed=int(us * 3e6), transcendentals=0
        ),
        name=name,
    )(*args)
    return result if len(result) > 1 else result[0]


def place_of(order):
    pos1, pos2, mid = order // 32, (order // 8) % 4, order % 8
    row = (mid // 4) * 4 + (pos2 // 2) * 2 + pos1 // 2
    col = (mid % 4) * 4 + (pos2 % 2) * 2 + pos1 % 2
    return row, col


def widen(*blocks):
    return jnp.concatenate([block.astype(F32) for block in blocks], axis=1)


def rows_kernel(tokens, left, right, first_out, last_out):
    wide = widen(tokens[...], left[...], right[...])
    first_out[...] = wide[0:RADIUS].astype(BF)
    last_out[...] = wide[8 - RADIUS : 8].astype(BF)


def ordered(where, own, over_k, over_yh, over_both):
    blocks = [block[...] for block in (own, over_k, over_yh, over_both)]
    here = where[5] * 2 + where[4]
    result = []
    for i in range(4):
        row = blocks[3]
        for j in range(3):
            row = jnp.where(here == (i ^ j), blocks[j], row)
        result.append(row)
    return result


def join_kernel(where, own, over_k, over_yh, over_both, out):
    blocks = [block.astype(F32) for block in ordered(where, own, over_k, over_yh, over_both)]
    for k in range(2):
        out[k] = jnp.concatenate([blocks[k], blocks[2 + k]], axis=1).astype(BF)


def finest_kernel(
    where,
    tokens,
    left,
    right,
    top,
    bottom,
    scale,
    wk,
    wv,
    wq,
    wo,
    merge,
    split,
    resid_out,
    level1_out,
    band_out,
    split_out,
    resid_near,
    level1_near,
    sent,
):
    split_out[...] = split[...]
    wide = widen(tokens[...], left[...], right[...])
    floats = jnp.concatenate(
        [top[...].astype(F32), wide, bottom[...].astype(F32)], axis=0
    ).reshape(448, 384)
    mean = jnp.mean(floats * floats, axis=1, keepdims=True)
    normed = (floats * lax.rsqrt(mean + EPSILON) * scale[...]).astype(BF)
    keys = dot(normed, wk[...]).astype(BF)
    values = dot(normed, wv[...]).astype(BF)

    row, col = place_of(lax.broadcasted_iota(jnp.int32, (128, 448), 0))
    place = lax.broadcasted_iota(jnp.int32, (128, 448), 1)
    key_row, slot = place // 32 - RADIUS, place % 32
    key_col = jnp.where(slot < 16, slot, jnp.where(slot < 24, slot - 24, slot - 8))
    pick = ((key_row == row) & (slot == col)).astype(F32).astype(BF)
    mine = dot(pick, floats.astype(BF))
    queries = dot(dot(pick, normed).astype(BF), wq[...]).astype(BF)

    global_row, global_col = key_row + where[0], key_col + where[1]
    inside = (jnp.abs(key_row - row) <= RADIUS) & (jnp.abs(key_col - col) <= RADIUS)
    inside &= (global_row >= 0) & (global_row < where[2])
    inside &= (global_col >= 0) & (global_col < where[3])
    bias = jnp.where(inside, 0.0, LOWEST)

    lane = lax.broadcasted_iota(jnp.int32, (1, 128), 1)
    low = (lane < HEAD).astype(F32).astype(BF)
    high = (lane >= HEAD).astype(F32).astype(BF)
    blocks = []
    for pair in range(3):
        cut = slice(128 * pair, 128 * pair + 128)
        outs = []
        for half in (low, high):
            scores = dot_nt(queries[:, cut] * half, keys[:, cut]) * (1.0 / math.sqrt(HEAD)) + bias
            exps = jnp.exp(scores - jnp.max(scores, axis=1, keepdims=True))
            weights = (exps / jnp.sum(exps, axis=1, keepdims=True)).astype(BF)
            outs.append(dot(weights, values[:, cut]))
        blocks.append(jnp.where(lane < HEAD, outs[0], outs[1]))
    attended = jnp.concatenate(blocks, axis=1).astype(BF)
    resid = (mine + dot(attended, wo[...])).astype(BF)
    resid_near[...] = resid
    send_resid = pltpu.make_async_copy(resid_near, resid_out, sent.at[0])
    send_resid.start()
    level1 = jnp.zeros((32, 768), F32)
    for pos in range(4):
        level1 += dot(resid[32 * pos : 32 * pos + 32], merge[384 * pos : 384 * pos + 384, :])
    level1_near[...] = level1.astype(BF)
    send_level1 = pltpu.make_async_copy(level1_near, level1_out, sent.at[1])
    send_level1.start()
    grouped = jnp.concatenate([level1[8 * pos : 8 * pos + 8] for pos in range(4)], axis=1)
    band_out[...] = jnp.concatenate([grouped] * 8, axis=0).astype(BF)
    send_resid.wait()
    send_level1.wait()


def middle_kernel(band, weight, mid_out, copies_out):
    low = dot(band[:, 0:1536], weight[...])[:, 0:192]
    high = dot(band[:, 1536:3072], weight[...])[:, 192:384]
    mid = (low + high).astype(BF)
    mid_out[...] = mid
    copies_out[...] = jnp.concatenate([mid] * 8, axis=0)


def project_kernel(
    where, mids, gain, wq, wk, wv, own, over_k, over_yh, over_both, q_out, kv_out, split_out
):
    split_out[...] = jnp.concatenate(ordered(where, own, over_k, over_yh, over_both), axis=0)
    parts = [mids[64 * i : 64 * i + 64, :].astype(F32) for i in range(8)]
    total = jnp.zeros((64, 1), F32)
    for part in parts:
        total += jnp.sum(part * part, axis=1, keepdims=True)
    inverse = lax.rsqrt(total * (1.0 / 1536.0) + EPSILON)
    sums = [jnp.zeros((64, 192), F32) for _ in range(3)]
    for i, part in enumerate(parts):
        normed = (part * inverse * gain[i : i + 1, :]).astype(BF)
        for j, weight in enumerate((wq, wk, wv)):
            sums[j] += dot_nt(normed, weight[:, 192 * i : 192 * i + 192])
    queries, keys, values = sums
    q_out[...] = queries.astype(BF)
    both = jnp.concatenate([keys, values[:, 128:192], values[:, 0:128]], axis=1).astype(BF)
    kv_out[...] = jnp.concatenate([both] * 8, axis=0)


def attend_kernel(q_own, q_other, kv, own_out, other_out):
    queries = jnp.concatenate([q_own[...], q_other[...]], axis=0)
    lane = lax.broadcasted_iota(jnp.int32, (1, 128), 1)
    low = (lane < HEAD).astype(F32).astype(BF)
    high = (lane >= HEAD).astype(F32).astype(BF)
    first = queries[:, 0:128]
    third = jnp.concatenate([queries[:, 128:192], jnp.zeros((128, HEAD), BF)], axis=1)
    stats = jnp.zeros((128, 128), F32)
    nums = []
    for head in range(3):
        query = (first * low, first * high, third)[head]
        keys = kv[:, 128:256] if head == 2 else kv[:, 0:128]
        values = kv[:, 128:256] if head == 2 else kv[:, 256:384]
        scores = dot_nt(query, keys) * (1.0 / math.sqrt(HEAD))
        top = jnp.max(scores, axis=1, keepdims=True)
        exps = jnp.exp(scores - top)
        total = jnp.sum(exps, axis=1, keepdims=True)
        nums.append(dot(exps.astype(BF), values))
        stats = jnp.where(lane == head, top, stats)
        stats = jnp.where(lane == 8 + head, total, stats)
    result = jnp.concatenate(
        [jnp.where(lane < HEAD, nums[0], nums[1]), jnp.where(lane < HEAD, stats, nums[2])], axis=1
    )
    own_out[...] = result[0:64]
    other_out[...] = result[64:128]


def combine_kernel(mine, theirs, out2, parts_out):
    a, b = mine[...], theirs[...]
    factors = []
    for head in range(3):
        top_a, top_b = a[:, 128 + head : 129 + head], b[:, 128 + head : 129 + head]
        sum_a, sum_b = a[:, 136 + head : 137 + head], b[:, 136 + head : 137 + head]
        top = jnp.maximum(top_a, top_b)
        fade_a, fade_b = jnp.exp(top_a - top), jnp.exp(top_b - top)
        whole = 1.0 / (sum_a * fade_a + sum_b * fade_b)
        factors.append((fade_a * whole, fade_b * whole))
    lane = lax.broadcasted_iota(jnp.int32, (1, 128), 1)
    first_a = jnp.where(lane < HEAD, factors[0][0], factors[1][0])
    first_b = jnp.where(lane < HEAD, factors[0][1], factors[1][1])
    pair = (a[:, 0:128] * first_a + b[:, 0:128] * first_b).astype(BF)
    last = (a[:, 192:256] * factors[2][0] + b[:, 192:256] * factors[2][1]).astype(BF)
    result = dot(pair, out2[0:128, :]) + dot(last, out2[128:192, :])
    parts_out[...] = jnp.concatenate(
        [result[:, 192 * i : 192 * i + 192] for i in range(8)], axis=0
    ).astype(BF)


def lift_kernel(parts, mid, weight, up_out):
    sums = mid[...].astype(F32)
    for i in range(8):
        sums += parts[64 * i : 64 * i + 64, :].astype(F32)
    lifted = sums.astype(BF)
    for i in range(8):
        up_out[:, 384 * i : 384 * i + 384] = dot(lifted, weight[i]).astype(BF)


def last_kernel(parts, level1, resid, split, out):
    up = jnp.sum(parts[...].astype(F32).reshape(8, 8, 3072), axis=0)
    spread = jnp.concatenate([up[:, 768 * pos : 768 * pos + 768] for pos in range(4)], axis=0)
    lifted = (level1[...].astype(F32) + spread).astype(BF)
    zero = dot(lifted, split[...])
    rise = jnp.concatenate([zero[:, 384 * pos : 384 * pos + 384] for pos in range(4)], axis=0)
    result = (resid[...].astype(F32) + rise).astype(BF)
    place = lax.broadcasted_iota(jnp.int32, (128, 128), 0)
    row, col = place_of(lax.broadcasted_iota(jnp.int32, (128, 128), 1))
    back = ((place // 16 == row) & (place % 16 == col)).astype(F32).astype(BF)
    out[...] = dot(back, result).reshape(8, 16, 384).astype(BF)


def time_features(timestep, count):
    half_count = count // 2
    ladder = jnp.arange(half_count, dtype=F32)
    freqs = jnp.exp(-math.log(10000.0) * ladder / half_count)
    angles = timestep.astype(F32)[0] * freqs
    return jnp.concatenate([jnp.cos(angles), jnp.sin(angles)])


def on_device(
    tokens,
    timestep,
    time_weight,
    query0,
    key0,
    value0,
    out0,
    merge_one,
    merge_two,
    gain_two,
    query2,
    key2,
    value2,
    out2,
    split_two,
    split_one,
):
    shaped = jax.ShapeDtypeStruct
    left = lax.ppermute(tokens[:, 8:16], COL, shift(COL, 1))
    right = lax.ppermute(tokens[:, 0:8], COL, shift(COL, -1))
    first, last = call(
        rows_kernel, [shaped((RADIUS, 32, 384), BF)] * 2, (tokens, left, right), 1, name="rows"
    )
    top = lax.ppermute(last, ROW, shift(ROW, 1))
    bottom = lax.ppermute(first, ROW, shift(ROW, -1))

    condition = jnp.dot(
        time_features(timestep, FREQ)[None, :], time_weight, precision=lax.Precision.HIGHEST
    )
    where = jnp.stack(
        [
            lax.axis_index(ROW) * 8,
            lax.axis_index(COL) * 16,
            jnp.int32(8 * lax.axis_size(ROW)),
            jnp.int32(16 * lax.axis_size(COL)),
            lax.axis_index("k"),
            lax.axis_index("yh"),
            lax.axis_index(COL),
        ]
    ).astype(jnp.int32)
    def others(block):
        return (
            lax.ppermute(block, "k", swap("k")),
            lax.ppermute(block, "yh", swap("yh")),
            lax.ppermute(block, ("yh", "k"), [(0, 3), (1, 2), (2, 1), (3, 0)]),
        )

    perm = []
    for row in range(32):
        for col in range(8):
            yh, k = (row % 4) // 2, row % 2
            perm.append((row * 8 + col, ((yh * 8 + col) * 2 + k) * 8 + row // 4))
    split_block = lax.ppermute(split_two, ROW + COL, perm)

    weight = call(
        join_kernel,
        [shaped((2, 96, 384), BF)],
        (where, merge_two, *others(merge_two)),
        1,
        smem=(0,),
        name="join",
    )
    weight = lax.all_gather(weight.reshape(192, 384), "z", axis=0, tiled=True)

    resid, level1, band, split_block = call(
        finest_kernel,
        (
            shaped((128, 384), BF),
            shaped((32, 768), BF),
            shaped((64, 3072), BF),
            shaped((48, 384), BF),
        ),
        (
            where,
            tokens,
            left,
            right,
            top,
            bottom,
            1.0 + condition,
            key0,
            value0,
            query0,
            out0,
            merge_one,
            split_block,
        ),
        6,
        smem=(0,),
        out_far=(0, 1),
        scratch=(
            pltpu.VMEM((128, 384), BF),
            pltpu.VMEM((32, 768), BF),
            pltpu.SemaphoreType.DMA((2,)),
        ),
        name="finest",
    )
    band = exchange(band, COL)
    mid, mids, split_block = call(
        middle_kernel,
        (shaped((64, 192), BF), shaped((512, 192), BF)),
        (band, weight),
        2,
        through=(split_block,),
        name="middle",
    )
    mids = exchange(mids, COL)
    q, kv, split_block = call(
        project_kernel,
        (shaped((64, 192), BF), shaped((512, 384), BF), shaped((192, 384), BF)),
        (
            where,
            mids,
            gain_two.reshape(8, 192),
            query2.T,
            key2.T,
            value2.T,
            split_block,
            *others(split_block),
        ),
        2,
        smem=(0,),
        name="project",
    )
    split_block = lax.all_gather(split_block, "z", axis=0, tiled=False)
    q_other = lax.ppermute(q, "yh", swap("yh"))
    kv = exchange(kv, "z")
    kv = lax.all_gather(kv, "k", axis=0, tiled=True)
    own, other = call(
        attend_kernel,
        (shaped((64, 256), F32), shaped((64, 256), F32)),
        (q, q_other, kv),
        3,
        name="attend",
    )
    theirs = lax.ppermute(other, "yh", swap("yh"))
    parts = call(combine_kernel, [shaped((512, 192), BF)], (own, theirs, out2), 1, name="combine")
    parts = exchange(parts, COL)
    up = call(
        lift_kernel,
        [shaped((64, 3072), BF)],
        (parts, mid, split_block),
        1,
        name="lift",
    )
    up = exchange(up, COL)
    return call(
        last_kernel, [shaped((8, 16, 384), BF)], (up, level1, resid, split_one), 2, name="last"
    )


def solution(mesh):
    fine = Mesh(mesh.devices.reshape(2, 8, 2, 4, 2), ROW + COL)
    in_specs = (
        P(ROW, COL, None),
        P(),
        P(),
        P(),
        P(),
        P(),
        P(),
        P(),
        P(ROW, COL),
        P(),
        P(None, COL),
        P(None, COL),
        P(None, COL),
        P(COL, None),
        P(ROW, COL),
        P(),
    )
    return jax.shard_map(
        on_device, mesh=fine, in_specs=in_specs, out_specs=P(ROW, COL, None), check_vma=False
    )
```

```python
import functools
import math

import jax
import jax.numpy as jnp
from jax import lax
from jax.experimental import pallas as pl
from jax.experimental.pallas import tpu as pltpu
from jax.sharding import Mesh, PartitionSpec as P

HEAD = 64
RADIUS = 3
FREQ = 256
EPSILON = 1e-06
LOWEST = -1e30

ROW = ("yh", "z", "k")
COL = ("x", "yl")
BF = jnp.bfloat16
F32 = jnp.float32
MIB = 1 << 20


def shift(axis, step):
    count = lax.axis_size(axis)
    pairs = [(i, i + 1) for i in range(count - 1)]
    return pairs if step > 0 else [(b, a) for a, b in pairs]


def swap(axis):
    return [(0, 1), (1, 0)]


def exchange(block, axis):
    return lax.all_to_all(block, axis, split_axis=0, concat_axis=0, tiled=True)


def in_order(block, axis):
    other = lax.ppermute(block, axis, swap(axis))
    first = lax.axis_index(axis) == 0
    low = jnp.where(first, block, other)
    high = jnp.where(first, other, block)
    return jnp.concatenate([low, high], axis=0)


def copies(block, count):
    return jnp.broadcast_to(block[None], (count,) + block.shape).reshape(
        (count * block.shape[0],) + block.shape[1:]
    )


def dot(a, b):
    return jnp.dot(a, b, preferred_element_type=F32)


def dot_nt(a, b):
    return lax.dot_general(a, b, (((1,), (1,)), ((), ())), preferred_element_type=F32)


def call(body, out_shape, args, us, smem=(), far=(), through=(), scratch=(), name=None, vmem=16, out_far=()):
    ins, outs = len(args), len(out_shape)
    specs = [
        pl.BlockSpec(
            memory_space=pltpu.SMEM if i in smem else pltpu.HBM if i in far else pltpu.VMEM
        )
        for i in range(ins)
    ] + [pl.BlockSpec(memory_space=pl.ANY) for _ in through]
    out_specs = tuple(
        pl.BlockSpec(memory_space=pltpu.HBM if i in out_far else pltpu.VMEM) for i in range(outs)
    ) + tuple(
        pl.BlockSpec(memory_space=pl.ANY) for _ in through
    )
    out_shape = tuple(
        pltpu.HBM(a.shape, a.dtype) if i in out_far else a for i, a in enumerate(out_shape)
    ) + tuple(
        jax.ShapeDtypeStruct(a.shape, a.dtype) for a in through
    )
    args = tuple(args) + tuple(through)
    count = len(through)

    def kernel(*refs):
        body(*refs[:ins], *refs[ins + count : ins + count + outs], *refs[ins + 2 * count + outs :])

    result = pl.pallas_call(
        kernel,
        out_shape=out_shape,
        in_specs=specs,
        out_specs=out_specs,
        scratch_shapes=tuple(scratch),
        input_output_aliases={ins + i: outs + i for i in range(count)},
        compiler_params=pltpu.CompilerParams(vmem_limit_bytes=vmem * MIB),
        cost_estimate=pl.CostEstimate(
            flops=int(us * 1e9), bytes_accessed=int(us * 3e6), transcendentals=0
        ),
        name=name,
    )(*args)
    return result if len(result) > 1 else result[0]


def place_of(order):
    pos1, pos2, mid = order // 32, (order // 8) % 4, order % 8
    row = (mid // 4) * 4 + (pos2 // 2) * 2 + pos1 // 2
    col = (mid % 4) * 4 + (pos2 % 2) * 2 + pos1 % 2
    return row, col


def widen(*blocks):
    return jnp.concatenate([block.astype(F32) for block in blocks], axis=1)


def rows_kernel(tokens, left, right, first_out, last_out):
    wide = widen(tokens[...], left[...], right[...])
    first_out[...] = wide[0:RADIUS].astype(BF)
    last_out[...] = wide[8 - RADIUS : 8].astype(BF)


def copies_kernel(block, out):
    floats = block[...].astype(F32)
    packed = jnp.concatenate([floats[0:48], floats[48:96]], axis=1).astype(BF)
    for i in range(8):
        out[i] = packed


def finest_kernel(
    where,
    tokens,
    left,
    right,
    top,
    bottom,
    scale,
    wk_far,
    wv_far,
    wq_far,
    wo_far,
    merge_far,
    split,
    resid_out,
    level1_out,
    band_out,
    split_out,
    resid_near,
    level1_near,
    wk,
    wv,
    wq,
    wo,
    merge,
    sent,
    arrived,
):
    pairs = ((wk_far, wk), (wv_far, wv), (wq_far, wq), (wo_far, wo), (merge_far, merge))
    fetches = [
        pltpu.make_async_copy(far, near, arrived.at[i]) for i, (far, near) in enumerate(pairs)
    ]
    for fetch in fetches:
        fetch.start()
    split_out[...] = split[...]
    wide = widen(tokens[...], left[...], right[...])
    floats = jnp.concatenate(
        [top[...].astype(F32), wide, bottom[...].astype(F32)], axis=0
    ).reshape(448, 384)
    mean = jnp.mean(floats * floats, axis=1, keepdims=True)
    normed = (floats * lax.rsqrt(mean + EPSILON) * scale[...]).astype(BF)
    fetches[0].wait()
    keys = dot(normed, wk[...]).astype(BF)
    fetches[1].wait()
    values = dot(normed, wv[...]).astype(BF)

    row, col = place_of(lax.broadcasted_iota(jnp.int32, (128, 448), 0))
    place = lax.broadcasted_iota(jnp.int32, (128, 448), 1)
    key_row, slot = place // 32 - RADIUS, place % 32
    key_col = jnp.where(slot < 16, slot, jnp.where(slot < 24, slot - 24, slot - 8))
    pick = ((key_row == row) & (slot == col)).astype(F32).astype(BF)
    mine = dot(pick, floats.astype(BF))
    fetches[2].wait()
    queries = dot(dot(pick, normed).astype(BF), wq[...]).astype(BF)

    global_row, global_col = key_row + where[0], key_col + where[1]
    inside = (jnp.abs(key_row - row) <= RADIUS) & (jnp.abs(key_col - col) <= RADIUS)
    inside &= (global_row >= 0) & (global_row < where[2])
    inside &= (global_col >= 0) & (global_col < where[3])
    bias = jnp.where(inside, 0.0, LOWEST)

    lane = lax.broadcasted_iota(jnp.int32, (1, 128), 1)
    low = (lane < HEAD).astype(F32).astype(BF)
    high = (lane >= HEAD).astype(F32).astype(BF)
    blocks = []
    for pair in range(3):
        cut = slice(128 * pair, 128 * pair + 128)
        outs = []
        for half in (low, high):
            scores = dot_nt(queries[:, cut] * half, keys[:, cut]) * (1.0 / math.sqrt(HEAD)) + bias
            exps = jnp.exp(scores - jnp.max(scores, axis=1, keepdims=True))
            weights = (exps / jnp.sum(exps, axis=1, keepdims=True)).astype(BF)
            outs.append(dot(weights, values[:, cut]))
        blocks.append(jnp.where(lane < HEAD, outs[0], outs[1]))
    attended = jnp.concatenate(blocks, axis=1).astype(BF)
    fetches[3].wait()
    resid = (mine + dot(attended, wo[...])).astype(BF)
    resid_near[...] = resid
    send_resid = pltpu.make_async_copy(resid_near, resid_out, sent.at[0])
    send_resid.start()
    fetches[4].wait()
    level1 = jnp.zeros((32, 768), F32)
    for pos in range(4):
        level1 += dot(resid[32 * pos : 32 * pos + 32], merge[384 * pos : 384 * pos + 384, :])
    level1_near[...] = level1.astype(BF)
    send_level1 = pltpu.make_async_copy(level1_near, level1_out, sent.at[1])
    send_level1.start()
    grouped = jnp.concatenate([level1[8 * pos : 8 * pos + 8] for pos in range(4)], axis=1)
    band_out[...] = jnp.concatenate([grouped] * 8, axis=0).astype(BF)
    send_resid.wait()
    send_level1.wait()


def middle_kernel(where, band, own, over_k, over_yh, over_both, mid_out, copies_out):
    here = where[5] * 2 + where[4]
    blocks = []
    for yh in range(2):
        for z in range(8):
            for k in range(2):
                block = over_both[z]
                for j, ref in enumerate((own, over_k, over_yh)):
                    block = jnp.where(here == ((yh * 2 + k) ^ j), ref[z], block)
                blocks += [block[:, 0:192], block[:, 192:384]]
    mid = dot(band[...], jnp.concatenate(blocks, axis=0)).astype(BF)
    mid_out[...] = mid
    copies_out[...] = jnp.concatenate([mid] * 8, axis=0)


def project_kernel(mids, gain, wq, wk, wv, split, over_yh, q_out, kv_out, split_out):
    split_out[...] = jnp.concatenate([split[...], over_yh[...]], axis=0)
    parts = [mids[64 * i : 64 * i + 64, :].astype(F32) for i in range(8)]
    total = jnp.zeros((64, 1), F32)
    for part in parts:
        total += jnp.sum(part * part, axis=1, keepdims=True)
    inverse = lax.rsqrt(total * (1.0 / 1536.0) + EPSILON)
    sums = [jnp.zeros((64, 192), F32) for _ in range(3)]
    for i, part in enumerate(parts):
        normed = (part * inverse * gain[i : i + 1, :]).astype(BF)
        for j, weight in enumerate((wq, wk, wv)):
            sums[j] += dot_nt(normed, weight[:, 192 * i : 192 * i + 192])
    queries, keys, values = sums
    q_out[...] = queries.astype(BF)
    both = jnp.concatenate([keys, values[:, 128:192], values[:, 0:128]], axis=1).astype(BF)
    kv_out[...] = jnp.concatenate([both] * 8, axis=0)


def attend_kernel(q_own, q_other, kv, *refs):
    (own_out, other_out, stack_out), blocks = refs[8:], refs[:8]
    for i, block in enumerate(blocks):
        stack_out[i] = block[...]
    queries = jnp.concatenate([q_own[...], q_other[...]], axis=0)
    lane = lax.broadcasted_iota(jnp.int32, (1, 128), 1)
    low = (lane < HEAD).astype(F32).astype(BF)
    high = (lane >= HEAD).astype(F32).astype(BF)
    first = queries[:, 0:128]
    third = jnp.concatenate([queries[:, 128:192], jnp.zeros((128, HEAD), BF)], axis=1)
    stats = jnp.zeros((128, 128), F32)
    nums = []
    for head in range(3):
        query = (first * low, first * high, third)[head]
        keys = kv[:, 128:256] if head == 2 else kv[:, 0:128]
        values = kv[:, 128:256] if head == 2 else kv[:, 256:384]
        scores = dot_nt(query, keys) * (1.0 / math.sqrt(HEAD))
        top = jnp.max(scores, axis=1, keepdims=True)
        exps = jnp.exp(scores - top)
        total = jnp.sum(exps, axis=1, keepdims=True)
        nums.append(dot(exps.astype(BF), values))
        stats = jnp.where(lane == head, top, stats)
        stats = jnp.where(lane == 8 + head, total, stats)
    result = jnp.concatenate(
        [jnp.where(lane < HEAD, nums[0], nums[1]), jnp.where(lane < HEAD, stats, nums[2])], axis=1
    )
    own_out[...] = result[0:64]
    other_out[...] = result[64:128]


def combine_kernel(mine, theirs, out2, parts_out):
    a, b = mine[...], theirs[...]
    factors = []
    for head in range(3):
        top_a, top_b = a[:, 128 + head : 129 + head], b[:, 128 + head : 129 + head]
        sum_a, sum_b = a[:, 136 + head : 137 + head], b[:, 136 + head : 137 + head]
        top = jnp.maximum(top_a, top_b)
        fade_a, fade_b = jnp.exp(top_a - top), jnp.exp(top_b - top)
        whole = 1.0 / (sum_a * fade_a + sum_b * fade_b)
        factors.append((fade_a * whole, fade_b * whole))
    lane = lax.broadcasted_iota(jnp.int32, (1, 128), 1)
    first_a = jnp.where(lane < HEAD, factors[0][0], factors[1][0])
    first_b = jnp.where(lane < HEAD, factors[0][1], factors[1][1])
    pair = (a[:, 0:128] * first_a + b[:, 0:128] * first_b).astype(BF)
    last = (a[:, 192:256] * factors[2][0] + b[:, 192:256] * factors[2][1]).astype(BF)
    result = dot(pair, out2[0:128, :]) + dot(last, out2[128:192, :])
    parts_out[...] = jnp.concatenate(
        [result[:, 192 * i : 192 * i + 192] for i in range(8)], axis=0
    ).astype(BF)


def lift_kernel(where, parts, mid, weight, over_k, up_out):
    sums = mid[...].astype(F32)
    for i in range(8):
        sums += parts[64 * i : 64 * i + 64, :].astype(F32)
    lifted = sums.astype(BF)
    here = where[5] * 2 + where[4]
    source = lax.broadcasted_iota(jnp.int32, (192, 192), 0)
    target = lax.broadcasted_iota(jnp.int32, (192, 192), 1)
    turn = (target // 48) % 2 * 2 + target // 96
    same = (source // 48 == turn ^ here) & (source % 48 == target % 48)
    lifted = dot(lifted, same.astype(F32).astype(BF)).astype(BF)
    for i in range(8):
        rows = jnp.concatenate([weight[i], over_k[i]], axis=0)
        column = pl.multiple_of(lax.rem(where[6] + 8 - i, 8) * 384, 128)
        up_out[:, pl.ds(column, 384)] = dot(lifted, rows).astype(BF)


def last_kernel(parts, level1, resid, split, out):
    up = jnp.sum(parts[...].astype(F32).reshape(8, 8, 3072), axis=0)
    spread = jnp.concatenate([up[:, 768 * pos : 768 * pos + 768] for pos in range(4)], axis=0)
    lifted = (level1[...].astype(F32) + spread).astype(BF)
    zero = dot(lifted, split[...])
    rise = jnp.concatenate([zero[:, 384 * pos : 384 * pos + 384] for pos in range(4)], axis=0)
    result = (resid[...].astype(F32) + rise).astype(BF)
    place = lax.broadcasted_iota(jnp.int32, (128, 128), 0)
    row, col = place_of(lax.broadcasted_iota(jnp.int32, (128, 128), 1))
    back = ((place // 16 == row) & (place % 16 == col)).astype(F32).astype(BF)
    out[...] = dot(back, result).reshape(8, 16, 384).astype(BF)


def time_features(timestep, count):
    half_count = count // 2
    ladder = jnp.arange(half_count, dtype=F32)
    freqs = jnp.exp(-math.log(10000.0) * ladder / half_count)
    angles = timestep.astype(F32)[0] * freqs
    return jnp.concatenate([jnp.cos(angles), jnp.sin(angles)])


def on_device(
    tokens,
    timestep,
    time_weight,
    query0,
    key0,
    value0,
    out0,
    merge_one,
    merge_two,
    gain_two,
    query2,
    key2,
    value2,
    out2,
    split_two,
    split_one,
):
    shaped = jax.ShapeDtypeStruct
    left = lax.ppermute(tokens[:, 8:16], COL, shift(COL, 1))
    right = lax.ppermute(tokens[:, 0:8], COL, shift(COL, -1))
    first, last = call(
        rows_kernel, [shaped((RADIUS, 32, 384), BF)] * 2, (tokens, left, right), 1, name="rows"
    )
    top = lax.ppermute(last, ROW, shift(ROW, 1))
    bottom = lax.ppermute(first, ROW, shift(ROW, -1))

    condition = jnp.dot(
        time_features(timestep, FREQ)[None, :], time_weight, precision=lax.Precision.HIGHEST
    )
    where = jnp.stack(
        [
            lax.axis_index(ROW) * 8,
            lax.axis_index(COL) * 16,
            jnp.int32(8 * lax.axis_size(ROW)),
            jnp.int32(16 * lax.axis_size(COL)),
            lax.axis_index("k"),
            lax.axis_index("yh"),
            lax.axis_index("z"),
        ]
    ).astype(jnp.int32)
    def others(block):
        return (
            lax.ppermute(block, "k", swap("k")),
            lax.ppermute(block, "yh", swap("yh")),
            lax.ppermute(block, ("yh", "k"), [(0, 3), (1, 2), (2, 1), (3, 0)]),
        )

    perm = []
    for row in range(32):
        for col in range(8):
            yh, k = (row % 4) // 2, row % 2
            perm.append((row * 8 + col, ((yh * 8 + col) * 2 + k) * 8 + row // 4))
    split_block = lax.ppermute(split_two, ROW + COL, perm)

    merge_own = call(copies_kernel, [shaped((8, 48, 384), BF)], (merge_two,), 1, name="copies")
    merge_own = exchange(merge_own, "z")
    merge_yh = lax.ppermute(merge_own, "yh", swap("yh"))
    resid, level1, band, split_block = call(
        finest_kernel,
        (
            shaped((128, 384), BF),
            shaped((32, 768), BF),
            shaped((64, 3072), BF),
            shaped((48, 384), BF),
        ),
        (
            where,
            tokens,
            left,
            right,
            top,
            bottom,
            1.0 + condition,
            key0,
            value0,
            query0,
            out0,
            merge_one,
            split_block,
        ),
        6,
        smem=(0,),
        out_far=(0, 1),
        scratch=(
            pltpu.VMEM((128, 384), BF),
            pltpu.VMEM((32, 768), BF),
            *[pltpu.VMEM((384, 384), BF) for _ in range(4)],
            pltpu.VMEM((1536, 768), BF),
            pltpu.SemaphoreType.DMA((2,)),
            pltpu.SemaphoreType.DMA((5,)),
        ),
        far=(7, 8, 9, 10, 11),
        vmem=60,
        name="finest",
    )
    band = exchange(band, COL)
    over_yh = lax.ppermute(split_block, "yh", swap("yh"))
    merge_k, merge_both = [lax.ppermute(w, "k", swap("k")) for w in (merge_own, merge_yh)]
    mid, mids = call(
        middle_kernel,
        (shaped((64, 192), BF), shaped((512, 192), BF)),
        (where, band, merge_own, merge_k, merge_yh, merge_both),
        2,
        smem=(0,),
        name="middle",
    )
    mids = exchange(mids, COL)
    q, kv, split_block = call(
        project_kernel,
        (shaped((64, 192), BF), shaped((512, 384), BF), shaped((96, 384), BF)),
        (
            mids,
            gain_two.reshape(8, 192),
            query2.T,
            key2.T,
            value2.T,
            split_block,
            over_yh,
        ),
        2,
        name="project",
    )
    split_blocks = [split_block] + [
        lax.ppermute(split_block, "z", [(i, (i + step) % 8) for i in range(8)])
        for step in range(1, 8)
    ]
    q_other = lax.ppermute(q, "yh", swap("yh"))
    kv = exchange(kv, "z")
    kv = lax.all_gather(kv, "k", axis=0, tiled=True)
    own, other, split_block = call(
        attend_kernel,
        (shaped((64, 256), F32), shaped((64, 256), F32), shaped((8, 96, 384), BF)),
        (q, q_other, kv, *split_blocks),
        3,
        name="attend",
    )
    theirs = lax.ppermute(other, "yh", swap("yh"))
    split_other = lax.ppermute(split_block, "k", swap("k"))
    parts = call(combine_kernel, [shaped((512, 192), BF)], (own, theirs, out2), 1, name="combine")
    parts = exchange(parts, COL)
    up = call(
        lift_kernel,
        [shaped((64, 3072), BF)],
        (where, parts, mid, split_block, split_other),
        1,
        smem=(0,),
        name="lift",
    )
    up = exchange(up, COL)
    return call(
        last_kernel, [shaped((8, 16, 384), BF)], (up, level1, resid, split_one), 2, name="last"
    )


def solution(mesh):
    fine = Mesh(mesh.devices.reshape(2, 8, 2, 4, 2), ROW + COL)
    in_specs = (
        P(ROW, COL, None),
        P(),
        P(),
        P(),
        P(),
        P(),
        P(),
        P(),
        P(ROW, COL),
        P(),
        P(None, COL),
        P(None, COL),
        P(None, COL),
        P(COL, None),
        P(ROW, COL),
        P(),
    )
    return jax.shard_map(
        on_device, mesh=fine, in_specs=in_specs, out_specs=P(ROW, COL, None), check_vma=False
    )
```

```python
import functools
import math

import jax
import jax.numpy as jnp
from jax import lax
from jax.experimental import pallas as pl
from jax.experimental.pallas import tpu as pltpu
from jax.sharding import Mesh, PartitionSpec as P

HEAD = 64
RADIUS = 3
FREQ = 256
EPSILON = 1e-06
LOWEST = -1e30

ROW = ("yh", "z", "k")
COL = ("x", "yl")
BF = jnp.bfloat16
F32 = jnp.float32
MIB = 1 << 20


def shift(axis, step):
    count = lax.axis_size(axis)
    pairs = [(i, i + 1) for i in range(count - 1)]
    return pairs if step > 0 else [(b, a) for a, b in pairs]


def swap(axis):
    return [(0, 1), (1, 0)]


def exchange(block, axis):
    return lax.all_to_all(block, axis, split_axis=0, concat_axis=0, tiled=True)


def in_order(block, axis):
    other = lax.ppermute(block, axis, swap(axis))
    first = lax.axis_index(axis) == 0
    low = jnp.where(first, block, other)
    high = jnp.where(first, other, block)
    return jnp.concatenate([low, high], axis=0)


def copies(block, count):
    return jnp.broadcast_to(block[None], (count,) + block.shape).reshape(
        (count * block.shape[0],) + block.shape[1:]
    )


def dot(a, b):
    return jnp.dot(a, b, preferred_element_type=F32)


def dot_nt(a, b):
    return lax.dot_general(a, b, (((1,), (1,)), ((), ())), preferred_element_type=F32)


def call(body, out_shape, args, us, smem=(), far=(), through=(), scratch=(), name=None, vmem=16, out_far=()):
    ins, outs = len(args), len(out_shape)
    specs = [
        pl.BlockSpec(
            memory_space=pltpu.SMEM if i in smem else pltpu.HBM if i in far else pltpu.VMEM
        )
        for i in range(ins)
    ] + [pl.BlockSpec(memory_space=pl.ANY) for _ in through]
    out_specs = tuple(
        pl.BlockSpec(memory_space=pltpu.HBM if i in out_far else pltpu.VMEM) for i in range(outs)
    ) + tuple(
        pl.BlockSpec(memory_space=pl.ANY) for _ in through
    )
    out_shape = tuple(
        pltpu.HBM(a.shape, a.dtype) if i in out_far else a for i, a in enumerate(out_shape)
    ) + tuple(
        jax.ShapeDtypeStruct(a.shape, a.dtype) for a in through
    )
    args = tuple(args) + tuple(through)
    count = len(through)

    def kernel(*refs):
        body(*refs[:ins], *refs[ins + count : ins + count + outs], *refs[ins + 2 * count + outs :])

    result = pl.pallas_call(
        kernel,
        out_shape=out_shape,
        in_specs=specs,
        out_specs=out_specs,
        scratch_shapes=tuple(scratch),
        input_output_aliases={ins + i: outs + i for i in range(count)},
        compiler_params=pltpu.CompilerParams(vmem_limit_bytes=vmem * MIB),
        cost_estimate=pl.CostEstimate(
            flops=int(us * 1e9), bytes_accessed=int(us * 3e6), transcendentals=0
        ),
        name=name,
    )(*args)
    return result if len(result) > 1 else result[0]


def place_of(order):
    pos1, pos2, mid = order // 32, (order // 8) % 4, order % 8
    row = (mid // 4) * 4 + (pos2 // 2) * 2 + pos1 // 2
    col = (mid % 4) * 4 + (pos2 % 2) * 2 + pos1 % 2
    return row, col


def widen(*blocks):
    return jnp.concatenate([block.astype(F32) for block in blocks], axis=1)


def rows_kernel(tokens, left, right, first_out, last_out):
    wide = widen(tokens[...], left[...], right[...])
    first_out[...] = wide[0:RADIUS].astype(BF)
    last_out[...] = wide[8 - RADIUS : 8].astype(BF)


def copies_kernel(block, out):
    floats = block[...].astype(F32)
    packed = jnp.concatenate([floats[0:48], floats[48:96]], axis=1).astype(BF)
    for i in range(8):
        out[i] = packed


def finest_kernel(
    where,
    tokens,
    left,
    right,
    top,
    bottom,
    scale,
    wk_far,
    wv_far,
    wq_far,
    wo_far,
    merge_far,
    split,
    split_yh,
    resid_out,
    level1_out,
    band_out,
    split_out,
    resid_near,
    level1_near,
    wk,
    wv,
    wq,
    wo,
    merge,
    sent,
    arrived,
):
    pairs = ((wk_far, wk), (wv_far, wv), (wq_far, wq), (wo_far, wo), (merge_far, merge))
    fetches = [
        pltpu.make_async_copy(far, near, arrived.at[i]) for i, (far, near) in enumerate(pairs)
    ]
    for fetch in fetches:
        fetch.start()
    split_out[...] = jnp.concatenate([split[...], split_yh[...]], axis=0)
    wide = widen(tokens[...], left[...], right[...])
    floats = jnp.concatenate(
        [top[...].astype(F32), wide, bottom[...].astype(F32)], axis=0
    ).reshape(448, 384)
    mean = jnp.mean(floats * floats, axis=1, keepdims=True)
    normed = (floats * lax.rsqrt(mean + EPSILON) * scale[...]).astype(BF)
    fetches[0].wait()
    keys = dot(normed, wk[...]).astype(BF)
    fetches[1].wait()
    values = dot(normed, wv[...]).astype(BF)

    row, col = place_of(lax.broadcasted_iota(jnp.int32, (128, 448), 0))
    place = lax.broadcasted_iota(jnp.int32, (128, 448), 1)
    key_row, slot = place // 32 - RADIUS, place % 32
    key_col = jnp.where(slot < 16, slot, jnp.where(slot < 24, slot - 24, slot - 8))
    pick = ((key_row == row) & (slot == col)).astype(F32).astype(BF)
    mine = dot(pick, floats.astype(BF))
    fetches[2].wait()
    queries = dot(dot(pick, normed).astype(BF), wq[...]).astype(BF)

    global_row, global_col = key_row + where[0], key_col + where[1]
    inside = (jnp.abs(key_row - row) <= RADIUS) & (jnp.abs(key_col - col) <= RADIUS)
    inside &= (global_row >= 0) & (global_row < where[2])
    inside &= (global_col >= 0) & (global_col < where[3])
    bias = jnp.where(inside, 0.0, LOWEST)

    lane = lax.broadcasted_iota(jnp.int32, (1, 128), 1)
    low = (lane < HEAD).astype(F32).astype(BF)
    high = (lane >= HEAD).astype(F32).astype(BF)
    blocks = []
    for pair in range(3):
        cut = slice(128 * pair, 128 * pair + 128)
        outs = []
        for half in (low, high):
            scores = dot_nt(queries[:, cut] * half, keys[:, cut]) * (1.0 / math.sqrt(HEAD)) + bias
            exps = jnp.exp(scores - jnp.max(scores, axis=1, keepdims=True))
            weights = (exps / jnp.sum(exps, axis=1, keepdims=True)).astype(BF)
            outs.append(dot(weights, values[:, cut]))
        blocks.append(jnp.where(lane < HEAD, outs[0], outs[1]))
    attended = jnp.concatenate(blocks, axis=1).astype(BF)
    fetches[3].wait()
    resid = (mine + dot(attended, wo[...])).astype(BF)
    resid_near[...] = resid
    send_resid = pltpu.make_async_copy(resid_near, resid_out, sent.at[0])
    send_resid.start()
    fetches[4].wait()
    level1 = jnp.zeros((32, 768), F32)
    for pos in range(4):
        level1 += dot(resid[32 * pos : 32 * pos + 32], merge[384 * pos : 384 * pos + 384, :])
    level1_near[...] = level1.astype(BF)
    send_level1 = pltpu.make_async_copy(level1_near, level1_out, sent.at[1])
    send_level1.start()
    grouped = jnp.concatenate([level1[8 * pos : 8 * pos + 8] for pos in range(4)], axis=1)
    band_out[...] = jnp.concatenate([grouped] * 8, axis=0).astype(BF)
    send_resid.wait()
    send_level1.wait()


def middle_kernel(where, band, own, over_k, over_yh, over_both, *refs):
    mid_out, copies_out = refs[3:]
    here = where[5] * 2 + where[4]
    blocks = []
    for yh in range(2):
        for z in range(8):
            for k in range(2):
                block = over_both[z]
                for j, ref in enumerate((own, over_k, over_yh)):
                    block = jnp.where(here == ((yh * 2 + k) ^ j), ref[z], block)
                blocks += [block[:, 0:192], block[:, 192:384]]
    mid = dot(band[...], jnp.concatenate(blocks, axis=0)).astype(BF)
    mid_out[...] = mid
    copies_out[...] = jnp.concatenate([mid] * 8, axis=0)


def project_kernel(mids, gain, wq, wk, wv, *refs):
    q_out, kv_out = refs[4:]
    parts = [mids[64 * i : 64 * i + 64, :].astype(F32) for i in range(8)]
    total = jnp.zeros((64, 1), F32)
    for part in parts:
        total += jnp.sum(part * part, axis=1, keepdims=True)
    inverse = lax.rsqrt(total * (1.0 / 1536.0) + EPSILON)
    sums = [jnp.zeros((64, 192), F32) for _ in range(3)]
    for i, part in enumerate(parts):
        normed = (part * inverse * gain[i : i + 1, :]).astype(BF)
        for j, weight in enumerate((wq, wk, wv)):
            sums[j] += dot_nt(normed, weight[:, 192 * i : 192 * i + 192])
    queries, keys, values = sums
    q_out[...] = queries.astype(BF)
    both = jnp.concatenate([keys, values[:, 128:192], values[:, 0:128]], axis=1).astype(BF)
    kv_out[...] = jnp.concatenate([both] * 8, axis=0)


def attend_kernel(q_own, q_other, kv, *refs):
    (own_out, other_out, stack_out), blocks = refs[8:], refs[:8]
    for i, block in enumerate(blocks):
        stack_out[i] = block[...]
    queries = jnp.concatenate([q_own[...], q_other[...]], axis=0)
    lane = lax.broadcasted_iota(jnp.int32, (1, 128), 1)
    low = (lane < HEAD).astype(F32).astype(BF)
    high = (lane >= HEAD).astype(F32).astype(BF)
    first = queries[:, 0:128]
    third = jnp.concatenate([queries[:, 128:192], jnp.zeros((128, HEAD), BF)], axis=1)
    stats = jnp.zeros((128, 128), F32)
    nums = []
    for head in range(3):
        query = (first * low, first * high, third)[head]
        keys = kv[:, 128:256] if head == 2 else kv[:, 0:128]
        values = kv[:, 128:256] if head == 2 else kv[:, 256:384]
        scores = dot_nt(query, keys) * (1.0 / math.sqrt(HEAD))
        top = jnp.max(scores, axis=1, keepdims=True)
        exps = jnp.exp(scores - top)
        total = jnp.sum(exps, axis=1, keepdims=True)
        nums.append(dot(exps.astype(BF), values))
        stats = jnp.where(lane == head, top, stats)
        stats = jnp.where(lane == 8 + head, total, stats)
    result = jnp.concatenate(
        [jnp.where(lane < HEAD, nums[0], nums[1]), jnp.where(lane < HEAD, stats, nums[2])], axis=1
    )
    own_out[...] = result[0:64]
    other_out[...] = result[64:128]


def combine_kernel(mine, theirs, out2, parts_out):
    a, b = mine[...], theirs[...]
    factors = []
    for head in range(3):
        top_a, top_b = a[:, 128 + head : 129 + head], b[:, 128 + head : 129 + head]
        sum_a, sum_b = a[:, 136 + head : 137 + head], b[:, 136 + head : 137 + head]
        top = jnp.maximum(top_a, top_b)
        fade_a, fade_b = jnp.exp(top_a - top), jnp.exp(top_b - top)
        whole = 1.0 / (sum_a * fade_a + sum_b * fade_b)
        factors.append((fade_a * whole, fade_b * whole))
    lane = lax.broadcasted_iota(jnp.int32, (1, 128), 1)
    first_a = jnp.where(lane < HEAD, factors[0][0], factors[1][0])
    first_b = jnp.where(lane < HEAD, factors[0][1], factors[1][1])
    pair = (a[:, 0:128] * first_a + b[:, 0:128] * first_b).astype(BF)
    last = (a[:, 192:256] * factors[2][0] + b[:, 192:256] * factors[2][1]).astype(BF)
    result = dot(pair, out2[0:128, :]) + dot(last, out2[128:192, :])
    parts_out[...] = jnp.concatenate(
        [result[:, 192 * i : 192 * i + 192] for i in range(8)], axis=0
    ).astype(BF)


def lift_kernel(where, parts, mid, weight, over_k, up_out):
    sums = mid[...].astype(F32)
    for i in range(8):
        sums += parts[64 * i : 64 * i + 64, :].astype(F32)
    lifted = sums.astype(BF)
    here = where[5] * 2 + where[4]
    source = lax.broadcasted_iota(jnp.int32, (192, 192), 0)
    target = lax.broadcasted_iota(jnp.int32, (192, 192), 1)
    turn = (target // 48) % 2 * 2 + target // 96
    same = (source // 48 == turn ^ here) & (source % 48 == target % 48)
    lifted = dot(lifted, same.astype(F32).astype(BF)).astype(BF)
    for i in range(8):
        rows = jnp.concatenate([weight[i], over_k[i]], axis=0)
        column = pl.multiple_of(lax.rem(where[6] + 8 - i, 8) * 384, 128)
        up_out[:, pl.ds(column, 384)] = dot(lifted, rows).astype(BF)


def last_kernel(parts, level1, resid, split, out):
    up = jnp.sum(parts[...].astype(F32).reshape(8, 8, 3072), axis=0)
    spread = jnp.concatenate([up[:, 768 * pos : 768 * pos + 768] for pos in range(4)], axis=0)
    lifted = (level1[...].astype(F32) + spread).astype(BF)
    zero = dot(lifted, split[...])
    rise = jnp.concatenate([zero[:, 384 * pos : 384 * pos + 384] for pos in range(4)], axis=0)
    result = (resid[...].astype(F32) + rise).astype(BF)
    place = lax.broadcasted_iota(jnp.int32, (128, 128), 0)
    row, col = place_of(lax.broadcasted_iota(jnp.int32, (128, 128), 1))
    back = ((place // 16 == row) & (place % 16 == col)).astype(F32).astype(BF)
    out[...] = dot(back, result).reshape(8, 16, 384).astype(BF)


def time_features(timestep, count):
    half_count = count // 2
    ladder = jnp.arange(half_count, dtype=F32)
    freqs = jnp.exp(-math.log(10000.0) * ladder / half_count)
    angles = timestep.astype(F32)[0] * freqs
    return jnp.concatenate([jnp.cos(angles), jnp.sin(angles)])


def on_device(
    tokens,
    timestep,
    time_weight,
    query0,
    key0,
    value0,
    out0,
    merge_one,
    merge_two,
    gain_two,
    query2,
    key2,
    value2,
    out2,
    split_two,
    split_one,
):
    shaped = jax.ShapeDtypeStruct
    left = lax.ppermute(tokens[:, 8:16], COL, shift(COL, 1))
    right = lax.ppermute(tokens[:, 0:8], COL, shift(COL, -1))
    first, last = call(
        rows_kernel, [shaped((RADIUS, 32, 384), BF)] * 2, (tokens, left, right), 1, name="rows"
    )
    top = lax.ppermute(last, ROW, shift(ROW, 1))
    bottom = lax.ppermute(first, ROW, shift(ROW, -1))

    condition = jnp.dot(
        time_features(timestep, FREQ)[None, :], time_weight, precision=lax.Precision.HIGHEST
    )
    where = jnp.stack(
        [
            lax.axis_index(ROW) * 8,
            lax.axis_index(COL) * 16,
            jnp.int32(8 * lax.axis_size(ROW)),
            jnp.int32(16 * lax.axis_size(COL)),
            lax.axis_index("k"),
            lax.axis_index("yh"),
            lax.axis_index("z"),
        ]
    ).astype(jnp.int32)
    def others(block):
        return (
            lax.ppermute(block, "k", swap("k")),
            lax.ppermute(block, "yh", swap("yh")),
            lax.ppermute(block, ("yh", "k"), [(0, 3), (1, 2), (2, 1), (3, 0)]),
        )

    perm = []
    for row in range(32):
        for col in range(8):
            yh, k = (row % 4) // 2, row % 2
            perm.append((row * 8 + col, ((yh * 8 + col) * 2 + k) * 8 + row // 4))
    split_block = lax.ppermute(split_two, ROW + COL, perm)

    merge_own = call(copies_kernel, [shaped((8, 48, 384), BF)], (merge_two,), 1, name="copies")
    merge_own = exchange(merge_own, "z")
    merge_yh = lax.ppermute(merge_own, "yh", swap("yh"))
    resid, level1, band, split_block = call(
        finest_kernel,
        (
            shaped((128, 384), BF),
            shaped((32, 768), BF),
            shaped((64, 3072), BF),
            shaped((96, 384), BF),
        ),
        (
            where,
            tokens,
            left,
            right,
            top,
            bottom,
            1.0 + condition,
            key0,
            value0,
            query0,
            out0,
            merge_one,
            split_block,
            lax.ppermute(split_block, "yh", swap("yh")),
        ),
        6,
        smem=(0,),
        out_far=(0, 1),
        scratch=(
            pltpu.VMEM((128, 384), BF),
            pltpu.VMEM((32, 768), BF),
            *[pltpu.VMEM((384, 384), BF) for _ in range(4)],
            pltpu.VMEM((1536, 768), BF),
            pltpu.SemaphoreType.DMA((2,)),
            pltpu.SemaphoreType.DMA((5,)),
        ),
        far=(7, 8, 9, 10, 11),
        vmem=60,
        name="finest",
    )
    band = exchange(band, COL)
    split_blocks = [split_block] + [
        lax.ppermute(split_block, "z", [(i, (i + step) % 8) for i in range(8)])
        for step in range(1, 8)
    ]
    merge_k, merge_both = [lax.ppermute(w, "k", swap("k")) for w in (merge_own, merge_yh)]
    mid, mids = call(
        middle_kernel,
        (shaped((64, 192), BF), shaped((512, 192), BF)),
        (where, band, merge_own, merge_k, merge_yh, merge_both)
        + tuple(split_blocks[i] for i in (1, 2, 7)),
        2,
        smem=(0,),
        far=(6, 7, 8),
        name="middle",
    )
    mids = exchange(mids, COL)
    q, kv = call(
        project_kernel,
        (shaped((64, 192), BF), shaped((512, 384), BF)),
        (mids, gain_two.reshape(8, 192), query2.T, key2.T, value2.T, *split_blocks[3:7]),
        2,
        far=(5, 6, 7, 8),
        name="project",
    )
    q_other = lax.ppermute(q, "yh", swap("yh"))
    kv = exchange(kv, "z")
    kv = lax.all_gather(kv, "k", axis=0, tiled=True)
    own, other, split_block = call(
        attend_kernel,
        (shaped((64, 256), F32), shaped((64, 256), F32), shaped((8, 96, 384), BF)),
        (q, q_other, kv, *split_blocks),
        3,
        name="attend",
    )
    theirs = lax.ppermute(other, "yh", swap("yh"))
    split_other = lax.ppermute(split_block, "k", swap("k"))
    parts = call(combine_kernel, [shaped((512, 192), BF)], (own, theirs, out2), 1, name="combine")
    parts = exchange(parts, COL)
    up = call(
        lift_kernel,
        [shaped((64, 3072), BF)],
        (where, parts, mid, split_block, split_other),
        1,
        smem=(0,),
        name="lift",
    )
    up = exchange(up, COL)
    return call(
        last_kernel, [shaped((8, 16, 384), BF)], (up, level1, resid, split_one), 2, name="last"
    )


def solution(mesh):
    fine = Mesh(mesh.devices.reshape(2, 8, 2, 4, 2), ROW + COL)
    in_specs = (
        P(ROW, COL, None),
        P(),
        P(),
        P(),
        P(),
        P(),
        P(),
        P(),
        P(ROW, COL),
        P(),
        P(None, COL),
        P(None, COL),
        P(None, COL),
        P(COL, None),
        P(ROW, COL),
        P(),
    )
    return jax.shard_map(
        on_device, mesh=fine, in_specs=in_specs, out_specs=P(ROW, COL, None), check_vma=False
    )
```

```python
import functools
import math

import jax
import jax.numpy as jnp
from jax import lax
from jax.experimental import pallas as pl
from jax.experimental.pallas import tpu as pltpu
from jax.sharding import Mesh, PartitionSpec as P

HEAD = 64
RADIUS = 3
FREQ = 256
EPSILON = 1e-06
LOWEST = -1e30

ROW = ("yh", "z", "k")
COL = ("x", "yl")
BF = jnp.bfloat16
F32 = jnp.float32
MIB = 1 << 20


def shift(axis, step):
    count = lax.axis_size(axis)
    pairs = [(i, i + 1) for i in range(count - 1)]
    return pairs if step > 0 else [(b, a) for a, b in pairs]


def swap(axis):
    return [(0, 1), (1, 0)]


def exchange(block, axis):
    return lax.all_to_all(block, axis, split_axis=0, concat_axis=0, tiled=True)


def in_order(block, axis):
    other = lax.ppermute(block, axis, swap(axis))
    first = lax.axis_index(axis) == 0
    low = jnp.where(first, block, other)
    high = jnp.where(first, other, block)
    return jnp.concatenate([low, high], axis=0)


def copies(block, count):
    return jnp.broadcast_to(block[None], (count,) + block.shape).reshape(
        (count * block.shape[0],) + block.shape[1:]
    )


def dot(a, b):
    return jnp.dot(a, b, preferred_element_type=F32)


def dot_nt(a, b):
    return lax.dot_general(a, b, (((1,), (1,)), ((), ())), preferred_element_type=F32)


def call(body, out_shape, args, us, smem=(), far=(), through=(), scratch=(), name=None, vmem=16, out_far=()):
    ins, outs = len(args), len(out_shape)
    specs = [
        pl.BlockSpec(
            memory_space=pltpu.SMEM if i in smem else pltpu.HBM if i in far else pltpu.VMEM
        )
        for i in range(ins)
    ] + [pl.BlockSpec(memory_space=pl.ANY) for _ in through]
    out_specs = tuple(
        pl.BlockSpec(memory_space=pltpu.HBM if i in out_far else pltpu.VMEM) for i in range(outs)
    ) + tuple(
        pl.BlockSpec(memory_space=pl.ANY) for _ in through
    )
    out_shape = tuple(
        pltpu.HBM(a.shape, a.dtype) if i in out_far else a for i, a in enumerate(out_shape)
    ) + tuple(
        jax.ShapeDtypeStruct(a.shape, a.dtype) for a in through
    )
    args = tuple(args) + tuple(through)
    count = len(through)

    def kernel(*refs):
        body(*refs[:ins], *refs[ins + count : ins + count + outs], *refs[ins + 2 * count + outs :])

    result = pl.pallas_call(
        kernel,
        out_shape=out_shape,
        in_specs=specs,
        out_specs=out_specs,
        scratch_shapes=tuple(scratch),
        input_output_aliases={ins + i: outs + i for i in range(count)},
        compiler_params=pltpu.CompilerParams(vmem_limit_bytes=vmem * MIB),
        cost_estimate=pl.CostEstimate(
            flops=int(us * 1e9), bytes_accessed=int(us * 3e6), transcendentals=0
        ),
        name=name,
    )(*args)
    return result if len(result) > 1 else result[0]


def place_of(order):
    pos1, pos2, mid = order // 32, (order // 8) % 4, order % 8
    row = (mid // 4) * 4 + (pos2 // 2) * 2 + pos1 // 2
    col = (mid % 4) * 4 + (pos2 % 2) * 2 + pos1 % 2
    return row, col


def widen(*blocks):
    return jnp.concatenate([block.astype(F32) for block in blocks], axis=1)


def rows_kernel(tokens, left, right, first_out, last_out):
    wide = widen(tokens[...], left[...], right[...])
    first_out[...] = wide[0:RADIUS].astype(BF)
    last_out[...] = wide[8 - RADIUS : 8].astype(BF)


def copies_kernel(block, out):
    floats = block[...].astype(F32)
    packed = jnp.concatenate([floats[0:48], floats[48:96]], axis=1).astype(BF)
    for i in range(8):
        out[i] = packed


def finest_kernel(
    where,
    tokens,
    left,
    right,
    top,
    bottom,
    scale,
    wk_far,
    wv_far,
    wq_far,
    wo_far,
    merge_far,
    split,
    resid_out,
    level1_out,
    band_out,
    split_out,
    resid_near,
    level1_near,
    wk,
    wv,
    wq,
    wo,
    merge,
    sent,
    arrived,
):
    pairs = ((wk_far, wk), (wv_far, wv), (wq_far, wq), (wo_far, wo), (merge_far, merge))
    fetches = [
        pltpu.make_async_copy(far, near, arrived.at[i]) for i, (far, near) in enumerate(pairs)
    ]
    for fetch in fetches:
        fetch.start()
    split_out[...] = split[...]
    wide = widen(tokens[...], left[...], right[...])
    floats = jnp.concatenate(
        [top[...].astype(F32), wide, bottom[...].astype(F32)], axis=0
    ).reshape(448, 384)
    mean = jnp.mean(floats * floats, axis=1, keepdims=True)
    normed = (floats * lax.rsqrt(mean + EPSILON) * scale[...]).astype(BF)
    fetches[0].wait()
    keys = dot(normed, wk[...]).astype(BF)
    fetches[1].wait()
    values = dot(normed, wv[...]).astype(BF)

    row, col = place_of(lax.broadcasted_iota(jnp.int32, (128, 448), 0))
    place = lax.broadcasted_iota(jnp.int32, (128, 448), 1)
    key_row, slot = place // 32 - RADIUS, place % 32
    key_col = jnp.where(slot < 16, slot, jnp.where(slot < 24, slot - 24, slot - 8))
    pick = ((key_row == row) & (slot == col)).astype(F32).astype(BF)
    mine = dot(pick, floats.astype(BF))
    fetches[2].wait()
    queries = dot(dot(pick, normed).astype(BF), wq[...]).astype(BF)

    global_row, global_col = key_row + where[0], key_col + where[1]
    inside = (jnp.abs(key_row - row) <= RADIUS) & (jnp.abs(key_col - col) <= RADIUS)
    inside &= (global_row >= 0) & (global_row < where[2])
    inside &= (global_col >= 0) & (global_col < where[3])
    bias = jnp.where(inside, 0.0, LOWEST)

    lane = lax.broadcasted_iota(jnp.int32, (1, 128), 1)
    low = (lane < HEAD).astype(F32).astype(BF)
    high = (lane >= HEAD).astype(F32).astype(BF)
    blocks = []
    for pair in range(3):
        cut = slice(128 * pair, 128 * pair + 128)
        outs = []
        for half in (low, high):
            scores = dot_nt(queries[:, cut] * half, keys[:, cut]) * (1.0 / math.sqrt(HEAD)) + bias
            exps = jnp.exp(scores - jnp.max(scores, axis=1, keepdims=True))
            weights = (exps / jnp.sum(exps, axis=1, keepdims=True)).astype(BF)
            outs.append(dot(weights, values[:, cut]))
        blocks.append(jnp.where(lane < HEAD, outs[0], outs[1]))
    attended = jnp.concatenate(blocks, axis=1).astype(BF)
    fetches[3].wait()
    resid = (mine + dot(attended, wo[...])).astype(BF)
    resid_near[...] = resid
    send_resid = pltpu.make_async_copy(resid_near, resid_out, sent.at[0])
    send_resid.start()
    fetches[4].wait()
    level1 = jnp.zeros((32, 768), F32)
    for pos in range(4):
        level1 += dot(resid[32 * pos : 32 * pos + 32], merge[384 * pos : 384 * pos + 384, :])
    level1_near[...] = level1.astype(BF)
    send_level1 = pltpu.make_async_copy(level1_near, level1_out, sent.at[1])
    send_level1.start()
    grouped = jnp.concatenate([level1[8 * pos : 8 * pos + 8] for pos in range(4)], axis=1)
    band_out[...] = jnp.concatenate([grouped] * 8, axis=0).astype(BF)
    send_resid.wait()
    send_level1.wait()


def middle_kernel(where, band, own, over_k, over_yh, over_both, mid_out, copies_out):
    here = where[5] * 2 + where[4]
    blocks = []
    for yh in range(2):
        for z in range(8):
            for k in range(2):
                block = over_both[z]
                for j, ref in enumerate((own, over_k, over_yh)):
                    block = jnp.where(here == ((yh * 2 + k) ^ j), ref[z], block)
                blocks += [block[:, 0:192], block[:, 192:384]]
    mid = dot(band[...], jnp.concatenate(blocks, axis=0)).astype(BF)
    mid_out[...] = mid
    copies_out[...] = jnp.concatenate([mid] * 8, axis=0)


def project_kernel(mids, gain, wq, wk, wv, split, over_yh, q_out, kv_out):
    parts = [mids[64 * i : 64 * i + 64, :].astype(F32) for i in range(8)]
    total = jnp.zeros((64, 1), F32)
    for part in parts:
        total += jnp.sum(part * part, axis=1, keepdims=True)
    inverse = lax.rsqrt(total * (1.0 / 1536.0) + EPSILON)
    sums = [jnp.zeros((64, 192), F32) for _ in range(3)]
    for i, part in enumerate(parts):
        normed = (part * inverse * gain[i : i + 1, :]).astype(BF)
        for j, weight in enumerate((wq, wk, wv)):
            sums[j] += dot_nt(normed, weight[:, 192 * i : 192 * i + 192])
    queries, keys, values = sums
    q_out[...] = queries.astype(BF)
    both = jnp.concatenate([keys, values[:, 128:192], values[:, 0:128]], axis=1).astype(BF)
    rows = jnp.concatenate([both, split[...], over_yh[...]], axis=0)
    for i in range(8):
        kv_out[i] = rows


def attend_kernel(q_own, q_other, blocks, others, own_out, other_out):
    kv = jnp.concatenate([ref[i, 0:64, :] for ref in (blocks, others) for i in range(8)], axis=0)
    queries = jnp.concatenate([q_own[...], q_other[...]], axis=0)
    lane = lax.broadcasted_iota(jnp.int32, (1, 128), 1)
    low = (lane < HEAD).astype(F32).astype(BF)
    high = (lane >= HEAD).astype(F32).astype(BF)
    first = queries[:, 0:128]
    third = jnp.concatenate([queries[:, 128:192], jnp.zeros((128, HEAD), BF)], axis=1)
    stats = jnp.zeros((128, 128), F32)
    nums = []
    for head in range(3):
        query = (first * low, first * high, third)[head]
        keys = kv[:, 128:256] if head == 2 else kv[:, 0:128]
        values = kv[:, 128:256] if head == 2 else kv[:, 256:384]
        scores = dot_nt(query, keys) * (1.0 / math.sqrt(HEAD))
        top = jnp.max(scores, axis=1, keepdims=True)
        exps = jnp.exp(scores - top)
        total = jnp.sum(exps, axis=1, keepdims=True)
        nums.append(dot(exps.astype(BF), values))
        stats = jnp.where(lane == head, top, stats)
        stats = jnp.where(lane == 8 + head, total, stats)
    result = jnp.concatenate(
        [jnp.where(lane < HEAD, nums[0], nums[1]), jnp.where(lane < HEAD, stats, nums[2])], axis=1
    )
    own_out[...] = result[0:64]
    other_out[...] = result[64:128]


def combine_kernel(mine, theirs, out2, parts_out):
    a, b = mine[...], theirs[...]
    factors = []
    for head in range(3):
        top_a, top_b = a[:, 128 + head : 129 + head], b[:, 128 + head : 129 + head]
        sum_a, sum_b = a[:, 136 + head : 137 + head], b[:, 136 + head : 137 + head]
        top = jnp.maximum(top_a, top_b)
        fade_a, fade_b = jnp.exp(top_a - top), jnp.exp(top_b - top)
        whole = 1.0 / (sum_a * fade_a + sum_b * fade_b)
        factors.append((fade_a * whole, fade_b * whole))
    lane = lax.broadcasted_iota(jnp.int32, (1, 128), 1)
    first_a = jnp.where(lane < HEAD, factors[0][0], factors[1][0])
    first_b = jnp.where(lane < HEAD, factors[0][1], factors[1][1])
    pair = (a[:, 0:128] * first_a + b[:, 0:128] * first_b).astype(BF)
    last = (a[:, 192:256] * factors[2][0] + b[:, 192:256] * factors[2][1]).astype(BF)
    result = dot(pair, out2[0:128, :]) + dot(last, out2[128:192, :])
    parts_out[...] = jnp.concatenate(
        [result[:, 192 * i : 192 * i + 192] for i in range(8)], axis=0
    ).astype(BF)


def lift_kernel(where, parts, mid, blocks, others, up_out):
    sums = mid[...].astype(F32)
    for i in range(8):
        sums += parts[64 * i : 64 * i + 64, :].astype(F32)
    lifted = sums.astype(BF)
    source = lax.broadcasted_iota(jnp.int32, (192, 192), 0)
    target = lax.broadcasted_iota(jnp.int32, (192, 192), 1)
    owner = (((target // 48) % 2) ^ where[5]) * 2 + ((target // 96) ^ where[4])
    same = (source // 48 == owner) & (source % 48 == target % 48)
    lifted = dot(lifted, same.astype(F32).astype(BF)).astype(BF)
    for i in range(8):
        rows = jnp.concatenate([blocks[i, 64:160, :], others[i, 64:160, :]], axis=0)
        up_out[:, 384 * i : 384 * i + 384] = dot(lifted, rows).astype(BF)


def last_kernel(parts, level1, resid, split, out):
    up = jnp.sum(parts[...].astype(F32).reshape(8, 8, 3072), axis=0)
    spread = jnp.concatenate([up[:, 768 * pos : 768 * pos + 768] for pos in range(4)], axis=0)
    lifted = (level1[...].astype(F32) + spread).astype(BF)
    zero = dot(lifted, split[...])
    rise = jnp.concatenate([zero[:, 384 * pos : 384 * pos + 384] for pos in range(4)], axis=0)
    result = (resid[...].astype(F32) + rise).astype(BF)
    place = lax.broadcasted_iota(jnp.int32, (128, 128), 0)
    row, col = place_of(lax.broadcasted_iota(jnp.int32, (128, 128), 1))
    back = ((place // 16 == row) & (place % 16 == col)).astype(F32).astype(BF)
    out[...] = dot(back, result).reshape(8, 16, 384).astype(BF)


def time_features(timestep, count):
    half_count = count // 2
    ladder = jnp.arange(half_count, dtype=F32)
    freqs = jnp.exp(-math.log(10000.0) * ladder / half_count)
    angles = timestep.astype(F32)[0] * freqs
    return jnp.concatenate([jnp.cos(angles), jnp.sin(angles)])


def on_device(
    tokens,
    timestep,
    time_weight,
    query0,
    key0,
    value0,
    out0,
    merge_one,
    merge_two,
    gain_two,
    query2,
    key2,
    value2,
    out2,
    split_two,
    split_one,
):
    shaped = jax.ShapeDtypeStruct
    left = lax.ppermute(tokens[:, 8:16], COL, shift(COL, 1))
    right = lax.ppermute(tokens[:, 0:8], COL, shift(COL, -1))
    first, last = call(
        rows_kernel, [shaped((RADIUS, 32, 384), BF)] * 2, (tokens, left, right), 1, name="rows"
    )
    top = lax.ppermute(last, ROW, shift(ROW, 1))
    bottom = lax.ppermute(first, ROW, shift(ROW, -1))

    condition = jnp.dot(
        time_features(timestep, FREQ)[None, :], time_weight, precision=lax.Precision.HIGHEST
    )
    where = jnp.stack(
        [
            lax.axis_index(ROW) * 8,
            lax.axis_index(COL) * 16,
            jnp.int32(8 * lax.axis_size(ROW)),
            jnp.int32(16 * lax.axis_size(COL)),
            lax.axis_index("k"),
            lax.axis_index("yh"),
            lax.axis_index("z"),
        ]
    ).astype(jnp.int32)
    def others(block):
        return (
            lax.ppermute(block, "k", swap("k")),
            lax.ppermute(block, "yh", swap("yh")),
            lax.ppermute(block, ("yh", "k"), [(0, 3), (1, 2), (2, 1), (3, 0)]),
        )

    perm = []
    for row in range(32):
        for col in range(8):
            yh, k = (row % 4) // 2, row % 2
            perm.append((row * 8 + col, ((yh * 8 + col) * 2 + k) * 8 + row // 4))
    split_block = lax.ppermute(split_two, ROW + COL, perm)

    merge_own = call(copies_kernel, [shaped((8, 48, 384), BF)], (merge_two,), 1, name="copies")
    merge_own = exchange(merge_own, "z")
    merge_yh = lax.ppermute(merge_own, "yh", swap("yh"))
    resid, level1, band, split_block = call(
        finest_kernel,
        (
            shaped((128, 384), BF),
            shaped((32, 768), BF),
            shaped((64, 3072), BF),
            shaped((48, 384), BF),
        ),
        (
            where,
            tokens,
            left,
            right,
            top,
            bottom,
            1.0 + condition,
            key0,
            value0,
            query0,
            out0,
            merge_one,
            split_block,
        ),
        6,
        smem=(0,),
        out_far=(0, 1),
        scratch=(
            pltpu.VMEM((128, 384), BF),
            pltpu.VMEM((32, 768), BF),
            *[pltpu.VMEM((384, 384), BF) for _ in range(4)],
            pltpu.VMEM((1536, 768), BF),
            pltpu.SemaphoreType.DMA((2,)),
            pltpu.SemaphoreType.DMA((5,)),
        ),
        far=(7, 8, 9, 10, 11),
        vmem=60,
        name="finest",
    )
    band = exchange(band, COL)
    over_yh = lax.ppermute(split_block, "yh", swap("yh"))
    merge_k, merge_both = [lax.ppermute(w, "k", swap("k")) for w in (merge_own, merge_yh)]
    mid, mids = call(
        middle_kernel,
        (shaped((64, 192), BF), shaped((512, 192), BF)),
        (where, band, merge_own, merge_k, merge_yh, merge_both),
        2,
        smem=(0,),
        name="middle",
    )
    mids = exchange(mids, COL)
    q, kv = call(
        project_kernel,
        (shaped((64, 192), BF), shaped((8, 160, 384), BF)),
        (
            mids,
            gain_two.reshape(8, 192),
            query2.T,
            key2.T,
            value2.T,
            split_block,
            over_yh,
        ),
        2,
        name="project",
    )
    q_other = lax.ppermute(q, "yh", swap("yh"))
    kv = exchange(kv, "z")
    kv_other = lax.ppermute(kv, "k", swap("k"))
    own, other = call(
        attend_kernel,
        (shaped((64, 256), F32), shaped((64, 256), F32)),
        (q, q_other, kv, kv_other),
        3,
        name="attend",
    )
    theirs = lax.ppermute(other, "yh", swap("yh"))
    parts = call(combine_kernel, [shaped((512, 192), BF)], (own, theirs, out2), 1, name="combine")
    parts = exchange(parts, COL)
    up = call(
        lift_kernel,
        [shaped((64, 3072), BF)],
        (where, parts, mid, kv, kv_other),
        1,
        smem=(0,),
        name="lift",
    )
    up = exchange(up, COL)
    return call(
        last_kernel, [shaped((8, 16, 384), BF)], (up, level1, resid, split_one), 2, name="last"
    )


def solution(mesh):
    fine = Mesh(mesh.devices.reshape(2, 8, 2, 4, 2), ROW + COL)
    in_specs = (
        P(ROW, COL, None),
        P(),
        P(),
        P(),
        P(),
        P(),
        P(),
        P(),
        P(ROW, COL),
        P(),
        P(None, COL),
        P(None, COL),
        P(None, COL),
        P(COL, None),
        P(ROW, COL),
        P(),
    )
    return jax.shard_map(
        on_device, mesh=fine, in_specs=in_specs, out_specs=P(ROW, COL, None), check_vma=False
    )
```

```python
import functools
import math

import jax
import jax.numpy as jnp
from jax import lax
from jax.experimental import pallas as pl
from jax.experimental.pallas import tpu as pltpu
from jax.sharding import Mesh, PartitionSpec as P

HEAD = 64
RADIUS = 3
FREQ = 256
EPSILON = 1e-06
LOWEST = -1e30

ROW = ("yh", "z", "k")
COL = ("x", "yl")
BF = jnp.bfloat16
F32 = jnp.float32
MIB = 1 << 20


def shift(axis, step):
    count = lax.axis_size(axis)
    pairs = [(i, i + 1) for i in range(count - 1)]
    return pairs if step > 0 else [(b, a) for a, b in pairs]


def swap(axis):
    return [(0, 1), (1, 0)]


def exchange(block, axis):
    return lax.all_to_all(block, axis, split_axis=0, concat_axis=0, tiled=True)


def in_order(block, axis):
    other = lax.ppermute(block, axis, swap(axis))
    first = lax.axis_index(axis) == 0
    low = jnp.where(first, block, other)
    high = jnp.where(first, other, block)
    return jnp.concatenate([low, high], axis=0)


def copies(block, count):
    return jnp.broadcast_to(block[None], (count,) + block.shape).reshape(
        (count * block.shape[0],) + block.shape[1:]
    )


def dot(a, b):
    return jnp.dot(a, b, preferred_element_type=F32)


def dot_nt(a, b):
    return lax.dot_general(a, b, (((1,), (1,)), ((), ())), preferred_element_type=F32)


def call(body, out_shape, args, us, smem=(), far=(), through=(), scratch=(), name=None, vmem=16, out_far=()):
    ins, outs = len(args), len(out_shape)
    specs = [
        pl.BlockSpec(
            memory_space=pltpu.SMEM if i in smem else pltpu.HBM if i in far else pltpu.VMEM
        )
        for i in range(ins)
    ] + [pl.BlockSpec(memory_space=pl.ANY) for _ in through]
    out_specs = tuple(
        pl.BlockSpec(memory_space=pltpu.HBM if i in out_far else pltpu.VMEM) for i in range(outs)
    ) + tuple(
        pl.BlockSpec(memory_space=pl.ANY) for _ in through
    )
    out_shape = tuple(
        pltpu.HBM(a.shape, a.dtype) if i in out_far else a for i, a in enumerate(out_shape)
    ) + tuple(
        jax.ShapeDtypeStruct(a.shape, a.dtype) for a in through
    )
    args = tuple(args) + tuple(through)
    count = len(through)

    def kernel(*refs):
        body(*refs[:ins], *refs[ins + count : ins + count + outs], *refs[ins + 2 * count + outs :])

    result = pl.pallas_call(
        kernel,
        out_shape=out_shape,
        in_specs=specs,
        out_specs=out_specs,
        scratch_shapes=tuple(scratch),
        input_output_aliases={ins + i: outs + i for i in range(count)},
        compiler_params=pltpu.CompilerParams(vmem_limit_bytes=vmem * MIB),
        cost_estimate=pl.CostEstimate(
            flops=int(us * 1e9), bytes_accessed=int(us * 3e6), transcendentals=0
        ),
        name=name,
    )(*args)
    return result if len(result) > 1 else result[0]


def place_of(order):
    pos1, pos2, mid = order // 32, (order // 8) % 4, order % 8
    row = (mid // 4) * 4 + (pos2 // 2) * 2 + pos1 // 2
    col = (mid % 4) * 4 + (pos2 % 2) * 2 + pos1 % 2
    return row, col


def widen(*blocks):
    return jnp.concatenate([block.astype(F32) for block in blocks], axis=1)


def rows_kernel(tokens, left, right, first_out, last_out):
    wide = widen(tokens[...], left[...], right[...])
    first_out[...] = wide[0:RADIUS].astype(BF)
    last_out[...] = wide[8 - RADIUS : 8].astype(BF)


def copies_kernel(block, out):
    floats = block[...].astype(F32)
    packed = jnp.concatenate([floats[0:48], floats[48:96]], axis=1).astype(BF)
    for i in range(8):
        out[i] = packed


def finest_kernel(
    where,
    tokens,
    left,
    right,
    top,
    bottom,
    scale,
    wk_far,
    wv_far,
    wq_far,
    wo_far,
    merge_far,
    split,
    resid_out,
    level1_out,
    band_out,
    split_out,
    resid_near,
    level1_near,
    wk,
    wv,
    wq,
    wo,
    merge,
    sent,
    arrived,
):
    pairs = ((wk_far, wk), (wv_far, wv), (wq_far, wq), (wo_far, wo), (merge_far, merge))
    fetches = [
        pltpu.make_async_copy(far, near, arrived.at[i]) for i, (far, near) in enumerate(pairs)
    ]
    for fetch in fetches:
        fetch.start()
    split_out[...] = split[...]
    wide = widen(tokens[...], left[...], right[...])
    floats = jnp.concatenate(
        [top[...].astype(F32), wide, bottom[...].astype(F32)], axis=0
    ).reshape(448, 384)
    mean = jnp.mean(floats * floats, axis=1, keepdims=True)
    normed = (floats * lax.rsqrt(mean + EPSILON) * scale[...]).astype(BF)
    fetches[0].wait()
    keys = dot(normed, wk[...]).astype(BF)
    fetches[1].wait()
    values = dot(normed, wv[...]).astype(BF)

    row, col = place_of(lax.broadcasted_iota(jnp.int32, (128, 448), 0))
    place = lax.broadcasted_iota(jnp.int32, (128, 448), 1)
    key_row, slot = place // 32 - RADIUS, place % 32
    key_col = jnp.where(slot < 16, slot, jnp.where(slot < 24, slot - 24, slot - 8))
    pick = ((key_row == row) & (slot == col)).astype(F32).astype(BF)
    mine = dot(pick, floats.astype(BF))
    fetches[2].wait()
    queries = dot(dot(pick, normed).astype(BF), wq[...]).astype(BF)

    global_row, global_col = key_row + where[0], key_col + where[1]
    inside = (jnp.abs(key_row - row) <= RADIUS) & (jnp.abs(key_col - col) <= RADIUS)
    inside &= (global_row >= 0) & (global_row < where[2])
    inside &= (global_col >= 0) & (global_col < where[3])
    bias = jnp.where(inside, 0.0, LOWEST)

    lane = lax.broadcasted_iota(jnp.int32, (1, 128), 1)
    low = (lane < HEAD).astype(F32).astype(BF)
    high = (lane >= HEAD).astype(F32).astype(BF)
    blocks = []
    for pair in range(3):
        cut = slice(128 * pair, 128 * pair + 128)
        outs = []
        for half in (low, high):
            scores = dot_nt(queries[:, cut] * half, keys[:, cut]) * (1.0 / math.sqrt(HEAD)) + bias
            exps = jnp.exp(scores - jnp.max(scores, axis=1, keepdims=True))
            weights = (exps / jnp.sum(exps, axis=1, keepdims=True)).astype(BF)
            outs.append(dot(weights, values[:, cut]))
        blocks.append(jnp.where(lane < HEAD, outs[0], outs[1]))
    attended = jnp.concatenate(blocks, axis=1).astype(BF)
    fetches[3].wait()
    resid = (mine + dot(attended, wo[...])).astype(BF)
    resid_near[...] = resid
    send_resid = pltpu.make_async_copy(resid_near, resid_out, sent.at[0])
    send_resid.start()
    fetches[4].wait()
    level1 = jnp.zeros((32, 768), F32)
    for pos in range(4):
        level1 += dot(resid[32 * pos : 32 * pos + 32], merge[384 * pos : 384 * pos + 384, :])
    level1_near[...] = level1.astype(BF)
    send_level1 = pltpu.make_async_copy(level1_near, level1_out, sent.at[1])
    send_level1.start()
    grouped = jnp.concatenate([level1[8 * pos : 8 * pos + 8] for pos in range(4)], axis=1)
    band_out[...] = jnp.concatenate([grouped] * 8, axis=0).astype(BF)
    send_resid.wait()
    send_level1.wait()


def middle_kernel(where, band, own, over_k, over_yh, over_both, mid_out, copies_out):
    here = where[5] * 2 + where[4]
    blocks = []
    for yh in range(2):
        for z in range(8):
            for k in range(2):
                block = over_both[z]
                for j, ref in enumerate((own, over_k, over_yh)):
                    block = jnp.where(here == ((yh * 2 + k) ^ j), ref[z], block)
                blocks += [block[:, 0:192], block[:, 192:384]]
    mid = dot(band[...], jnp.concatenate(blocks, axis=0)).astype(BF)
    mid_out[...] = mid
    copies_out[...] = jnp.concatenate([mid] * 8, axis=0)


def project_kernel(mids, gain, wq, wk, wv, split, over_yh, q_out, kv_out, split_out):
    split_out[...] = jnp.concatenate([split[...], over_yh[...]], axis=0)
    parts = [mids[64 * i : 64 * i + 64, :].astype(F32) for i in range(8)]
    total = jnp.zeros((64, 1), F32)
    for part in parts:
        total += jnp.sum(part * part, axis=1, keepdims=True)
    inverse = lax.rsqrt(total * (1.0 / 1536.0) + EPSILON)
    sums = [jnp.zeros((64, 192), F32) for _ in range(3)]
    for i, part in enumerate(parts):
        normed = (part * inverse * gain[i : i + 1, :]).astype(BF)
        for j, weight in enumerate((wq, wk, wv)):
            sums[j] += dot_nt(normed, weight[:, 192 * i : 192 * i + 192])
    queries, keys, values = sums
    q_out[...] = queries.astype(BF)
    both = jnp.concatenate([keys, values[:, 128:192], values[:, 0:128]], axis=1).astype(BF)
    kv_out[...] = jnp.concatenate([both] * 8, axis=0)


def attend_kernel(q_own, q_other, kv, own_out, other_out):
    queries = jnp.concatenate([q_own[...], q_other[...]], axis=0)
    lane = lax.broadcasted_iota(jnp.int32, (1, 128), 1)
    low = (lane < HEAD).astype(F32).astype(BF)
    high = (lane >= HEAD).astype(F32).astype(BF)
    first = queries[:, 0:128]
    third = jnp.concatenate([queries[:, 128:192], jnp.zeros((128, HEAD), BF)], axis=1)
    stats = jnp.zeros((128, 128), F32)
    nums = []
    for head in range(3):
        query = (first * low, first * high, third)[head]
        keys = kv[:, 128:256] if head == 2 else kv[:, 0:128]
        values = kv[:, 128:256] if head == 2 else kv[:, 256:384]
        scores = dot_nt(query, keys) * (1.0 / math.sqrt(HEAD))
        top = jnp.max(scores, axis=1, keepdims=True)
        exps = jnp.exp(scores - top)
        total = jnp.sum(exps, axis=1, keepdims=True)
        nums.append(dot(exps.astype(BF), values))
        stats = jnp.where(lane == head, top, stats)
        stats = jnp.where(lane == 8 + head, total, stats)
    result = jnp.concatenate(
        [jnp.where(lane < HEAD, nums[0], nums[1]), jnp.where(lane < HEAD, stats, nums[2])], axis=1
    )
    own_out[...] = result[0:64]
    other_out[...] = result[64:128]


def combine_kernel(mine, theirs, out2, *refs):
    (parts_out, stack_out), blocks = refs[8:], refs[:8]
    for i, block in enumerate(blocks):
        stack_out[i] = block[...]
    a, b = mine[...], theirs[...]
    factors = []
    for head in range(3):
        top_a, top_b = a[:, 128 + head : 129 + head], b[:, 128 + head : 129 + head]
        sum_a, sum_b = a[:, 136 + head : 137 + head], b[:, 136 + head : 137 + head]
        top = jnp.maximum(top_a, top_b)
        fade_a, fade_b = jnp.exp(top_a - top), jnp.exp(top_b - top)
        whole = 1.0 / (sum_a * fade_a + sum_b * fade_b)
        factors.append((fade_a * whole, fade_b * whole))
    lane = lax.broadcasted_iota(jnp.int32, (1, 128), 1)
    first_a = jnp.where(lane < HEAD, factors[0][0], factors[1][0])
    first_b = jnp.where(lane < HEAD, factors[0][1], factors[1][1])
    pair = (a[:, 0:128] * first_a + b[:, 0:128] * first_b).astype(BF)
    last = (a[:, 192:256] * factors[2][0] + b[:, 192:256] * factors[2][1]).astype(BF)
    result = dot(pair, out2[0:128, :]) + dot(last, out2[128:192, :])
    parts_out[...] = jnp.concatenate(
        [result[:, 192 * i : 192 * i + 192] for i in range(8)], axis=0
    ).astype(BF)


def lift_kernel(where, parts, mid, weight, over_k, up_out):
    sums = mid[...].astype(F32)
    for i in range(8):
        sums += parts[64 * i : 64 * i + 64, :].astype(F32)
    lifted = sums.astype(BF)
    here = where[5] * 2 + where[4]
    source = lax.broadcasted_iota(jnp.int32, (192, 192), 0)
    target = lax.broadcasted_iota(jnp.int32, (192, 192), 1)
    turn = (target // 48) % 2 * 2 + target // 96
    same = (source // 48 == turn ^ here) & (source % 48 == target % 48)
    lifted = dot(lifted, same.astype(F32).astype(BF)).astype(BF)
    for i in range(8):
        rows = jnp.concatenate([weight[i], over_k[i]], axis=0)
        column = pl.multiple_of(lax.rem(where[6] + 8 - i, 8) * 384, 128)
        up_out[:, pl.ds(column, 384)] = dot(lifted, rows).astype(BF)


def last_kernel(parts, level1, resid, split, out):
    up = jnp.sum(parts[...].astype(F32).reshape(8, 8, 3072), axis=0)
    spread = jnp.concatenate([up[:, 768 * pos : 768 * pos + 768] for pos in range(4)], axis=0)
    lifted = (level1[...].astype(F32) + spread).astype(BF)
    zero = dot(lifted, split[...])
    rise = jnp.concatenate([zero[:, 384 * pos : 384 * pos + 384] for pos in range(4)], axis=0)
    result = (resid[...].astype(F32) + rise).astype(BF)
    place = lax.broadcasted_iota(jnp.int32, (128, 128), 0)
    row, col = place_of(lax.broadcasted_iota(jnp.int32, (128, 128), 1))
    back = ((place // 16 == row) & (place % 16 == col)).astype(F32).astype(BF)
    out[...] = dot(back, result).reshape(8, 16, 384).astype(BF)


def time_features(timestep, count):
    half_count = count // 2
    ladder = jnp.arange(half_count, dtype=F32)
    freqs = jnp.exp(-math.log(10000.0) * ladder / half_count)
    angles = timestep.astype(F32)[0] * freqs
    return jnp.concatenate([jnp.cos(angles), jnp.sin(angles)])


def on_device(
    tokens,
    timestep,
    time_weight,
    query0,
    key0,
    value0,
    out0,
    merge_one,
    merge_two,
    gain_two,
    query2,
    key2,
    value2,
    out2,
    split_two,
    split_one,
):
    shaped = jax.ShapeDtypeStruct
    left = lax.ppermute(tokens[:, 8:16], COL, shift(COL, 1))
    right = lax.ppermute(tokens[:, 0:8], COL, shift(COL, -1))
    first, last = call(
        rows_kernel, [shaped((RADIUS, 32, 384), BF)] * 2, (tokens, left, right), 1, name="rows"
    )
    top = lax.ppermute(last, ROW, shift(ROW, 1))
    bottom = lax.ppermute(first, ROW, shift(ROW, -1))

    condition = jnp.dot(
        time_features(timestep, FREQ)[None, :], time_weight, precision=lax.Precision.HIGHEST
    )
    where = jnp.stack(
        [
            lax.axis_index(ROW) * 8,
            lax.axis_index(COL) * 16,
            jnp.int32(8 * lax.axis_size(ROW)),
            jnp.int32(16 * lax.axis_size(COL)),
            lax.axis_index("k"),
            lax.axis_index("yh"),
            lax.axis_index("z"),
        ]
    ).astype(jnp.int32)
    def others(block):
        return (
            lax.ppermute(block, "k", swap("k")),
            lax.ppermute(block, "yh", swap("yh")),
            lax.ppermute(block, ("yh", "k"), [(0, 3), (1, 2), (2, 1), (3, 0)]),
        )

    perm = []
    for row in range(32):
        for col in range(8):
            yh, k = (row % 4) // 2, row % 2
            perm.append((row * 8 + col, ((yh * 8 + col) * 2 + k) * 8 + row // 4))
    split_block = lax.ppermute(split_two, ROW + COL, perm)

    merge_own = call(copies_kernel, [shaped((8, 48, 384), BF)], (merge_two,), 1, name="copies")
    merge_own = exchange(merge_own, "z")
    merge_yh = lax.ppermute(merge_own, "yh", swap("yh"))
    resid, level1, band, split_block = call(
        finest_kernel,
        (
            shaped((128, 384), BF),
            shaped((32, 768), BF),
            shaped((64, 3072), BF),
            shaped((48, 384), BF),
        ),
        (
            where,
            tokens,
            left,
            right,
            top,
            bottom,
            1.0 + condition,
            key0,
            value0,
            query0,
            out0,
            merge_one,
            split_block,
        ),
        6,
        smem=(0,),
        out_far=(0, 1),
        scratch=(
            pltpu.VMEM((128, 384), BF),
            pltpu.VMEM((32, 768), BF),
            *[pltpu.VMEM((384, 384), BF) for _ in range(4)],
            pltpu.VMEM((1536, 768), BF),
            pltpu.SemaphoreType.DMA((2,)),
            pltpu.SemaphoreType.DMA((5,)),
        ),
        far=(7, 8, 9, 10, 11),
        vmem=60,
        name="finest",
    )
    band = exchange(band, COL)
    over_yh = lax.ppermute(split_block, "yh", swap("yh"))
    merge_k, merge_both = [lax.ppermute(w, "k", swap("k")) for w in (merge_own, merge_yh)]
    mid, mids = call(
        middle_kernel,
        (shaped((64, 192), BF), shaped((512, 192), BF)),
        (where, band, merge_own, merge_k, merge_yh, merge_both),
        2,
        smem=(0,),
        name="middle",
    )
    mids = exchange(mids, COL)
    q, kv, split_block = call(
        project_kernel,
        (shaped((64, 192), BF), shaped((512, 384), BF), shaped((96, 384), BF)),
        (
            mids,
            gain_two.reshape(8, 192),
            query2.T,
            key2.T,
            value2.T,
            split_block,
            over_yh,
        ),
        2,
        name="project",
    )
    split_blocks = [split_block] + [
        lax.ppermute(split_block, "z", [(i, (i + step) % 8) for i in range(8)])
        for step in range(1, 8)
    ]
    q_other = lax.ppermute(q, "yh", swap("yh"))
    kv = exchange(kv, "z")
    kv = lax.all_gather(kv, "k", axis=0, tiled=True)
    own, other = call(
        attend_kernel,
        (shaped((64, 256), F32), shaped((64, 256), F32)),
        (q, q_other, kv),
        3,
        name="attend",
    )
    theirs = lax.ppermute(other, "yh", swap("yh"))
    parts, split_block = call(
        combine_kernel,
        [shaped((512, 192), BF), shaped((8, 96, 384), BF)],
        (own, theirs, out2, *split_blocks),
        1,
        name="combine",
    )
    split_other = lax.ppermute(split_block, "k", swap("k"))
    parts = exchange(parts, COL)
    up = call(
        lift_kernel,
        [shaped((64, 3072), BF)],
        (where, parts, mid, split_block, split_other),
        1,
        smem=(0,),
        name="lift",
    )
    up = exchange(up, COL)
    return call(
        last_kernel, [shaped((8, 16, 384), BF)], (up, level1, resid, split_one), 2, name="last"
    )


def solution(mesh):
    fine = Mesh(mesh.devices.reshape(2, 8, 2, 4, 2), ROW + COL)
    in_specs = (
        P(ROW, COL, None),
        P(),
        P(),
        P(),
        P(),
        P(),
        P(),
        P(),
        P(ROW, COL),
        P(),
        P(None, COL),
        P(None, COL),
        P(None, COL),
        P(COL, None),
        P(ROW, COL),
        P(),
    )
    return jax.shard_map(
        on_device, mesh=fine, in_specs=in_specs, out_specs=P(ROW, COL, None), check_vma=False
    )
```

```python
import functools
import math

import jax
import jax.numpy as jnp
from jax import lax
from jax.experimental import pallas as pl
from jax.experimental.pallas import tpu as pltpu
from jax.sharding import Mesh, PartitionSpec as P

HEAD = 64
RADIUS = 3
FREQ = 256
EPSILON = 1e-06
LOWEST = -1e30

ROW = ("yh", "z", "k")
COL = ("x", "yl")
BF = jnp.bfloat16
F32 = jnp.float32
MIB = 1 << 20


def shift(axis, step):
    count = lax.axis_size(axis)
    pairs = [(i, i + 1) for i in range(count - 1)]
    return pairs if step > 0 else [(b, a) for a, b in pairs]


def swap(axis):
    return [(0, 1), (1, 0)]


def exchange(block, axis):
    return lax.all_to_all(block, axis, split_axis=0, concat_axis=0, tiled=True)


def in_order(block, axis):
    other = lax.ppermute(block, axis, swap(axis))
    first = lax.axis_index(axis) == 0
    low = jnp.where(first, block, other)
    high = jnp.where(first, other, block)
    return jnp.concatenate([low, high], axis=0)


def copies(block, count):
    return jnp.broadcast_to(block[None], (count,) + block.shape).reshape(
        (count * block.shape[0],) + block.shape[1:]
    )


def dot(a, b):
    return jnp.dot(a, b, preferred_element_type=F32)


def dot_nt(a, b):
    return lax.dot_general(a, b, (((1,), (1,)), ((), ())), preferred_element_type=F32)


def call(body, out_shape, args, us, smem=(), far=(), through=(), scratch=(), name=None, vmem=16, out_far=()):
    ins, outs = len(args), len(out_shape)
    specs = [
        pl.BlockSpec(
            memory_space=pltpu.SMEM if i in smem else pltpu.HBM if i in far else pltpu.VMEM
        )
        for i in range(ins)
    ] + [pl.BlockSpec(memory_space=pl.ANY) for _ in through]
    out_specs = tuple(
        pl.BlockSpec(memory_space=pltpu.HBM if i in out_far else pltpu.VMEM) for i in range(outs)
    ) + tuple(
        pl.BlockSpec(memory_space=pl.ANY) for _ in through
    )
    out_shape = tuple(
        pltpu.HBM(a.shape, a.dtype) if i in out_far else a for i, a in enumerate(out_shape)
    ) + tuple(
        jax.ShapeDtypeStruct(a.shape, a.dtype) for a in through
    )
    args = tuple(args) + tuple(through)
    count = len(through)

    def kernel(*refs):
        body(*refs[:ins], *refs[ins + count : ins + count + outs], *refs[ins + 2 * count + outs :])

    result = pl.pallas_call(
        kernel,
        out_shape=out_shape,
        in_specs=specs,
        out_specs=out_specs,
        scratch_shapes=tuple(scratch),
        input_output_aliases={ins + i: outs + i for i in range(count)},
        compiler_params=pltpu.CompilerParams(vmem_limit_bytes=vmem * MIB),
        cost_estimate=pl.CostEstimate(
            flops=int(us * 1e9), bytes_accessed=int(us * 3e6), transcendentals=0
        ),
        name=name,
    )(*args)
    return result if len(result) > 1 else result[0]


def place_of(order):
    pos1, pos2, mid = order // 32, (order // 8) % 4, order % 8
    row = (mid // 4) * 4 + (pos2 // 2) * 2 + pos1 // 2
    col = (mid % 4) * 4 + (pos2 % 2) * 2 + pos1 % 2
    return row, col


def widen(*blocks):
    return jnp.concatenate([block.astype(F32) for block in blocks], axis=1)


def rows_kernel(tokens, left, right, first_out, last_out):
    wide = widen(tokens[...], left[...], right[...])
    first_out[...] = wide[0:RADIUS].astype(BF)
    last_out[...] = wide[8 - RADIUS : 8].astype(BF)


def copies_kernel(block, out):
    floats = block[...].astype(F32)
    packed = jnp.concatenate([floats[0:48], floats[48:96]], axis=1).astype(BF)
    for i in range(8):
        out[i] = packed


def finest_kernel(
    where,
    tokens,
    left,
    right,
    top,
    bottom,
    scale,
    wk_far,
    wv_far,
    wq_far,
    wo_far,
    merge_far,
    split,
    resid_out,
    level1_out,
    band_out,
    split_out,
    resid_near,
    level1_near,
    wk,
    wv,
    wq,
    wo,
    merge,
    sent,
    arrived,
):
    pairs = ((wk_far, wk), (wv_far, wv), (wq_far, wq), (wo_far, wo), (merge_far, merge))
    fetches = [
        pltpu.make_async_copy(far, near, arrived.at[i]) for i, (far, near) in enumerate(pairs)
    ]
    for fetch in fetches[:3]:
        fetch.start()
    split_out[...] = split[...]
    wide = widen(tokens[...], left[...], right[...])
    floats = jnp.concatenate(
        [top[...].astype(F32), wide, bottom[...].astype(F32)], axis=0
    ).reshape(448, 384)
    mean = jnp.mean(floats * floats, axis=1, keepdims=True)
    normed = (floats * lax.rsqrt(mean + EPSILON) * scale[...]).astype(BF)
    fetches[0].wait()
    keys = dot(normed, wk[...]).astype(BF)
    fetches[1].wait()
    for fetch in fetches[3:]:
        fetch.start()
    values = dot(normed, wv[...]).astype(BF)

    row, col = place_of(lax.broadcasted_iota(jnp.int32, (128, 448), 0))
    place = lax.broadcasted_iota(jnp.int32, (128, 448), 1)
    key_row, slot = place // 32 - RADIUS, place % 32
    key_col = jnp.where(slot < 16, slot, jnp.where(slot < 24, slot - 24, slot - 8))
    pick = ((key_row == row) & (slot == col)).astype(F32).astype(BF)
    mine = dot(pick, floats.astype(BF))
    fetches[2].wait()
    queries = dot(dot(pick, normed).astype(BF), wq[...]).astype(BF)

    global_row, global_col = key_row + where[0], key_col + where[1]
    inside = (jnp.abs(key_row - row) <= RADIUS) & (jnp.abs(key_col - col) <= RADIUS)
    inside &= (global_row >= 0) & (global_row < where[2])
    inside &= (global_col >= 0) & (global_col < where[3])
    bias = jnp.where(inside, 0.0, LOWEST)

    lane = lax.broadcasted_iota(jnp.int32, (1, 128), 1)
    low = (lane < HEAD).astype(F32).astype(BF)
    high = (lane >= HEAD).astype(F32).astype(BF)
    blocks = []
    for pair in range(3):
        cut = slice(128 * pair, 128 * pair + 128)
        outs = []
        for half in (low, high):
            scores = dot_nt(queries[:, cut] * half, keys[:, cut]) * (1.0 / math.sqrt(HEAD)) + bias
            exps = jnp.exp(scores - jnp.max(scores, axis=1, keepdims=True))
            weights = (exps / jnp.sum(exps, axis=1, keepdims=True)).astype(BF)
            outs.append(dot(weights, values[:, cut]))
        blocks.append(jnp.where(lane < HEAD, outs[0], outs[1]))
    attended = jnp.concatenate(blocks, axis=1).astype(BF)
    fetches[3].wait()
    resid = (mine + dot(attended, wo[...])).astype(BF)
    resid_near[...] = resid
    send_resid = pltpu.make_async_copy(resid_near, resid_out, sent.at[0])
    send_resid.start()
    fetches[4].wait()
    level1 = jnp.zeros((32, 768), F32)
    for pos in range(4):
        level1 += dot(resid[32 * pos : 32 * pos + 32], merge[384 * pos : 384 * pos + 384, :])
    level1_near[...] = level1.astype(BF)
    send_level1 = pltpu.make_async_copy(level1_near, level1_out, sent.at[1])
    send_level1.start()
    grouped = jnp.concatenate([level1[8 * pos : 8 * pos + 8] for pos in range(4)], axis=1)
    band_out[...] = jnp.concatenate([grouped] * 8, axis=0).astype(BF)
    send_resid.wait()
    send_level1.wait()


def middle_kernel(where, band, own, over_k, over_yh, over_both, mid_out, copies_out):
    here = where[5] * 2 + where[4]
    blocks = []
    for yh in range(2):
        for z in range(8):
            for k in range(2):
                block = over_both[z]
                for j, ref in enumerate((own, over_k, over_yh)):
                    block = jnp.where(here == ((yh * 2 + k) ^ j), ref[z], block)
                blocks += [block[:, 0:192], block[:, 192:384]]
    mid = dot(band[...], jnp.concatenate(blocks, axis=0)).astype(BF)
    mid_out[...] = mid
    copies_out[...] = jnp.concatenate([mid] * 8, axis=0)


def project_kernel(mids, gain, wq, wk, wv, split, over_yh, q_out, kv_out, split_out):
    split_out[...] = jnp.concatenate([split[...], over_yh[...]], axis=0)
    parts = [mids[64 * i : 64 * i + 64, :].astype(F32) for i in range(8)]
    total = jnp.zeros((64, 1), F32)
    for part in parts:
        total += jnp.sum(part * part, axis=1, keepdims=True)
    inverse = lax.rsqrt(total * (1.0 / 1536.0) + EPSILON)
    sums = [jnp.zeros((64, 192), F32) for _ in range(3)]
    for i, part in enumerate(parts):
        normed = (part * inverse * gain[i : i + 1, :]).astype(BF)
        for j, weight in enumerate((wq, wk, wv)):
            sums[j] += dot_nt(normed, weight[:, 192 * i : 192 * i + 192])
    queries, keys, values = sums
    q_out[...] = queries.astype(BF)
    both = jnp.concatenate([keys, values[:, 128:192], values[:, 0:128]], axis=1).astype(BF)
    kv_out[...] = jnp.concatenate([both] * 8, axis=0)


def attend_kernel(q_own, q_other, kv, own_out, other_out):
    queries = jnp.concatenate([q_own[...], q_other[...]], axis=0)
    lane = lax.broadcasted_iota(jnp.int32, (1, 128), 1)
    low = (lane < HEAD).astype(F32).astype(BF)
    high = (lane >= HEAD).astype(F32).astype(BF)
    first = queries[:, 0:128]
    third = jnp.concatenate([queries[:, 128:192], jnp.zeros((128, HEAD), BF)], axis=1)
    stats = jnp.zeros((128, 128), F32)
    nums = []
    for head in range(3):
        query = (first * low, first * high, third)[head]
        keys = kv[:, 128:256] if head == 2 else kv[:, 0:128]
        values = kv[:, 128:256] if head == 2 else kv[:, 256:384]
        scores = dot_nt(query, keys) * (1.0 / math.sqrt(HEAD))
        top = jnp.max(scores, axis=1, keepdims=True)
        exps = jnp.exp(scores - top)
        total = jnp.sum(exps, axis=1, keepdims=True)
        nums.append(dot(exps.astype(BF), values))
        stats = jnp.where(lane == head, top, stats)
        stats = jnp.where(lane == 8 + head, total, stats)
    result = jnp.concatenate(
        [jnp.where(lane < HEAD, nums[0], nums[1]), jnp.where(lane < HEAD, stats, nums[2])], axis=1
    )
    own_out[...] = result[0:64]
    other_out[...] = result[64:128]


def combine_kernel(mine, theirs, out2, *refs):
    (parts_out, stack_out), blocks = refs[8:], refs[:8]
    for i, block in enumerate(blocks):
        stack_out[i] = block[...]
    a, b = mine[...], theirs[...]
    factors = []
    for head in range(3):
        top_a, top_b = a[:, 128 + head : 129 + head], b[:, 128 + head : 129 + head]
        sum_a, sum_b = a[:, 136 + head : 137 + head], b[:, 136 + head : 137 + head]
        top = jnp.maximum(top_a, top_b)
        fade_a, fade_b = jnp.exp(top_a - top), jnp.exp(top_b - top)
        whole = 1.0 / (sum_a * fade_a + sum_b * fade_b)
        factors.append((fade_a * whole, fade_b * whole))
    lane = lax.broadcasted_iota(jnp.int32, (1, 128), 1)
    first_a = jnp.where(lane < HEAD, factors[0][0], factors[1][0])
    first_b = jnp.where(lane < HEAD, factors[0][1], factors[1][1])
    pair = (a[:, 0:128] * first_a + b[:, 0:128] * first_b).astype(BF)
    last = (a[:, 192:256] * factors[2][0] + b[:, 192:256] * factors[2][1]).astype(BF)
    result = dot(pair, out2[0:128, :]) + dot(last, out2[128:192, :])
    parts_out[...] = jnp.concatenate(
        [result[:, 192 * i : 192 * i + 192] for i in range(8)], axis=0
    ).astype(BF)


def lift_kernel(where, parts, mid, weight, over_k, up_out):
    sums = mid[...].astype(F32)
    for i in range(8):
        sums += parts[64 * i : 64 * i + 64, :].astype(F32)
    lifted = sums.astype(BF)
    here = where[5] * 2 + where[4]
    source = lax.broadcasted_iota(jnp.int32, (192, 192), 0)
    target = lax.broadcasted_iota(jnp.int32, (192, 192), 1)
    turn = (target // 48) % 2 * 2 + target // 96
    same = (source // 48 == turn ^ here) & (source % 48 == target % 48)
    lifted = dot(lifted, same.astype(F32).astype(BF)).astype(BF)
    for i in range(8):
        rows = jnp.concatenate([weight[i], over_k[i]], axis=0)
        column = pl.multiple_of(lax.rem(where[6] + 8 - i, 8) * 384, 128)
        up_out[:, pl.ds(column, 384)] = dot(lifted, rows).astype(BF)


def last_kernel(parts, level1, resid, split, out):
    up = jnp.sum(parts[...].astype(F32).reshape(8, 8, 3072), axis=0)
    spread = jnp.concatenate([up[:, 768 * pos : 768 * pos + 768] for pos in range(4)], axis=0)
    lifted = (level1[...].astype(F32) + spread).astype(BF)
    zero = dot(lifted, split[...])
    rise = jnp.concatenate([zero[:, 384 * pos : 384 * pos + 384] for pos in range(4)], axis=0)
    result = (resid[...].astype(F32) + rise).astype(BF)
    place = lax.broadcasted_iota(jnp.int32, (128, 128), 0)
    row, col = place_of(lax.broadcasted_iota(jnp.int32, (128, 128), 1))
    back = ((place // 16 == row) & (place % 16 == col)).astype(F32).astype(BF)
    out[...] = dot(back, result).reshape(8, 16, 384).astype(BF)


def time_features(timestep, count):
    half_count = count // 2
    ladder = jnp.arange(half_count, dtype=F32)
    freqs = jnp.exp(-math.log(10000.0) * ladder / half_count)
    angles = timestep.astype(F32)[0] * freqs
    return jnp.concatenate([jnp.cos(angles), jnp.sin(angles)])


def on_device(
    tokens,
    timestep,
    time_weight,
    query0,
    key0,
    value0,
    out0,
    merge_one,
    merge_two,
    gain_two,
    query2,
    key2,
    value2,
    out2,
    split_two,
    split_one,
):
    shaped = jax.ShapeDtypeStruct
    left = lax.ppermute(tokens[:, 8:16], COL, shift(COL, 1))
    right = lax.ppermute(tokens[:, 0:8], COL, shift(COL, -1))
    first, last = call(
        rows_kernel, [shaped((RADIUS, 32, 384), BF)] * 2, (tokens, left, right), 1, name="rows"
    )
    top = lax.ppermute(last, ROW, shift(ROW, 1))
    bottom = lax.ppermute(first, ROW, shift(ROW, -1))

    condition = jnp.dot(
        time_features(timestep, FREQ)[None, :], time_weight, precision=lax.Precision.HIGHEST
    )
    where = jnp.stack(
        [
            lax.axis_index(ROW) * 8,
            lax.axis_index(COL) * 16,
            jnp.int32(8 * lax.axis_size(ROW)),
            jnp.int32(16 * lax.axis_size(COL)),
            lax.axis_index("k"),
            lax.axis_index("yh"),
            lax.axis_index("z"),
        ]
    ).astype(jnp.int32)
    def others(block):
        return (
            lax.ppermute(block, "k", swap("k")),
            lax.ppermute(block, "yh", swap("yh")),
            lax.ppermute(block, ("yh", "k"), [(0, 3), (1, 2), (2, 1), (3, 0)]),
        )

    perm = []
    for row in range(32):
        for col in range(8):
            yh, k = (row % 4) // 2, row % 2
            perm.append((row * 8 + col, ((yh * 8 + col) * 2 + k) * 8 + row // 4))
    split_block = lax.ppermute(split_two, ROW + COL, perm)

    merge_own = call(copies_kernel, [shaped((8, 48, 384), BF)], (merge_two,), 1, name="copies")
    merge_own = exchange(merge_own, "z")
    merge_yh = lax.ppermute(merge_own, "yh", swap("yh"))
    resid, level1, band, split_block = call(
        finest_kernel,
        (
            shaped((128, 384), BF),
            shaped((32, 768), BF),
            shaped((64, 3072), BF),
            shaped((48, 384), BF),
        ),
        (
            where,
            tokens,
            left,
            right,
            top,
            bottom,
            1.0 + condition,
            key0,
            value0,
            query0,
            out0,
            merge_one,
            split_block,
        ),
        6,
        smem=(0,),
        out_far=(0, 1),
        scratch=(
            pltpu.VMEM((128, 384), BF),
            pltpu.VMEM((32, 768), BF),
            *[pltpu.VMEM((384, 384), BF) for _ in range(4)],
            pltpu.VMEM((1536, 768), BF),
            pltpu.SemaphoreType.DMA((2,)),
            pltpu.SemaphoreType.DMA((5,)),
        ),
        far=(7, 8, 9, 10, 11),
        vmem=60,
        name="finest",
    )
    band = exchange(band, COL)
    over_yh = lax.ppermute(split_block, "yh", swap("yh"))
    merge_k, merge_both = [lax.ppermute(w, "k", swap("k")) for w in (merge_own, merge_yh)]
    mid, mids = call(
        middle_kernel,
        (shaped((64, 192), BF), shaped((512, 192), BF)),
        (where, band, merge_own, merge_k, merge_yh, merge_both),
        2,
        smem=(0,),
        name="middle",
    )
    mids = exchange(mids, COL)
    q, kv, split_block = call(
        project_kernel,
        (shaped((64, 192), BF), shaped((512, 384), BF), shaped((96, 384), BF)),
        (
            mids,
            gain_two.reshape(8, 192),
            query2.T,
            key2.T,
            value2.T,
            split_block,
            over_yh,
        ),
        2,
        name="project",
    )
    split_blocks = [split_block] + [
        lax.ppermute(split_block, "z", [(i, (i + step) % 8) for i in range(8)])
        for step in range(1, 8)
    ]
    q_other = lax.ppermute(q, "yh", swap("yh"))
    kv = exchange(kv, "z")
    kv = lax.all_gather(kv, "k", axis=0, tiled=True)
    own, other = call(
        attend_kernel,
        (shaped((64, 256), F32), shaped((64, 256), F32)),
        (q, q_other, kv),
        3,
        name="attend",
    )
    theirs = lax.ppermute(other, "yh", swap("yh"))
    parts, split_block = call(
        combine_kernel,
        [shaped((512, 192), BF), shaped((8, 96, 384), BF)],
        (own, theirs, out2, *split_blocks),
        1,
        name="combine",
    )
    split_other = lax.ppermute(split_block, "k", swap("k"))
    parts = exchange(parts, COL)
    up = call(
        lift_kernel,
        [shaped((64, 3072), BF)],
        (where, parts, mid, split_block, split_other),
        1,
        smem=(0,),
        name="lift",
    )
    up = exchange(up, COL)
    return call(
        last_kernel, [shaped((8, 16, 384), BF)], (up, level1, resid, split_one), 2, name="last"
    )


def solution(mesh):
    fine = Mesh(mesh.devices.reshape(2, 8, 2, 4, 2), ROW + COL)
    in_specs = (
        P(ROW, COL, None),
        P(),
        P(),
        P(),
        P(),
        P(),
        P(),
        P(),
        P(ROW, COL),
        P(),
        P(None, COL),
        P(None, COL),
        P(None, COL),
        P(COL, None),
        P(ROW, COL),
        P(),
    )
    return jax.shard_map(
        on_device, mesh=fine, in_specs=in_specs, out_specs=P(ROW, COL, None), check_vma=False
    )
```
